128 devices in a mesh: bx: 8 (over z, core), by: 16 (over y, x).
Axes of the slice: x: 4, y: 4, z: 4, core: 2. Of those that a mesh axis runs over, the one named last changes fastest.
Arguments:
- source: float32 [2048, 16384], P(('bx', 'by')), may hold values from -6 to 6
- coefficient: float32 [2048, 16384], P(('bx', 'by')), may hold values from 0.1 to 10
- initial_guess: float32 [2048, 16384], P(('bx', 'by')), may hold values from -6 to 6
- box_place: int32 [2048], replicated, may hold values from 0 to 2047, as said below
Outputs:
- solution: float32 [4, 1024, 8192], P(None, 'bx', 'by')
- residual: float32 [4, 1024, 8192], P(None, 'bx', 'by')
The draws below stay inside these ranges and needn't reach their ends.
Inputs may be any that keep to these rules, and one draw needn't show every extreme that they name: box_place is a permutation of the 2048 positions; the tile of device (i, j), at index i * 16 + j of bx+by, holds the positions with gx // 2 = i and gy // 8 = j. The boxes of rows d * 16 to (d + 1) * 16 - 1 place at most one box in any one tile; in fact each device sends exactly one box to each of 16 distinct tiles.
All inputs are finite; a program needn't handle non-finite values.
Results may differ from the reference program's by a relative error of at most 0.00002.
Values sent between devices are 32-bit elements; how exact they have to be, the bound alone decides.
A program may use at most 192 MiB of HBM per device.

```python
import math
import jax
import jax.numpy as jnp
from jax import lax

B = 64
BZ = 4
TX = 2
TY = 8
SWEEPS = 2
BOX_DEV = 16
CELLS = 16384
GX = 16
GY = 128
NBOX = 2048
N_BY = 16
DEVICES = 128


def draw_box_place(key, part):
    key = jax.random.fold_in(key, 11)
    key_order, key_offset, key_source, key_target = jax.random.split(key, 4)
    device_order = jax.random.permutation(key_order, DEVICES)
    device_rank = jnp.argsort(device_order)
    offsets = jax.random.permutation(key_offset, DEVICES)
    source_perm = jax.vmap(lambda subkey: jax.random.permutation(subkey, BOX_DEV))(jax.random.split(key_source, DEVICES))
    target_perm = jax.vmap(lambda subkey: jax.random.permutation(subkey, BOX_DEV))(jax.random.split(key_target, DEVICES))
    senders = jnp.arange(DEVICES, dtype=jnp.int32)[:, None]
    targets = device_order[(device_rank[senders] + offsets[source_perm % DEVICES]) % DEVICES]
    slots = target_perm[targets, source_perm]
    tile_x = targets // N_BY
    tile_y = targets % N_BY
    place_x = tile_x * TX + slots // TY
    place_y = tile_y * TY + slots % TY
    return (place_x * GY + place_y).reshape(-1).astype(jnp.int32)


def levels(stream_key, dims, cuts, least, top_value):
    factor_of = 1.0
    for dim, blocks in cuts:
        draws = jax.random.uniform(jax.random.fold_in(jax.random.fold_in(stream_key, 6), dim), (blocks,), jnp.float32, least / len(cuts), top_value / len(cuts))
        factor_of = factor_of * jnp.repeat(jnp.exp(draws), dims[dim] // blocks).reshape((-1,) + (1,) * (len(dims) - 1 - dim))
    return factor_of


def centred(rng, extent, width, reach, pieces=(), held_as=jnp.bfloat16):
    drawn = width * jax.random.normal(rng, extent, jnp.float32)
    if pieces:
        drawn = drawn * levels(rng, extent, pieces, -0.22, 0.18)
    return jnp.clip(drawn, -reach, reach).astype(held_as)


def setup_inputs(seed: int = 0) -> dict:
    key_of = jax.random.split(jax.random.key(seed), 5)
    return {
        "source": centred(key_of[0], (NBOX, CELLS), 1.0, 6.0, ((0, 128),), jnp.float32),
        "coefficient": jnp.clip(jnp.exp(math.log(10.0) - 4.6051702 * jax.random.uniform(key_of[1], (NBOX, CELLS), jnp.float32) ** levels(key_of[1], (NBOX, CELLS), ((0, 128),), -0.2, 0.2)), 0.1, 10.0),
        "initial_guess": centred(key_of[2], (NBOX, CELLS), 1.0, 6.0, ((0, 128),), jnp.float32),
        "box_place": draw_box_place(jax.random.fold_in(key_of[4], 71), 0),
    }


def to_grid(rows, box_place):
    placed = jnp.zeros_like(rows).at[box_place].set(rows)
    blocks = placed.reshape(GX, GY, BZ, B, B)
    return jnp.transpose(blocks, (2, 0, 3, 1, 4)).reshape(BZ, GX * B, GY * B)


def pad_plane(field):
    return jnp.pad(field, ((0, 0), (1, 1), (1, 1)))


def face_terms(beta_edged):
    padded = jnp.pad(beta_edged, ((1, 1), (0, 0), (0, 0)))
    centre = padded[1:-1, 1:-1, 1:-1]
    minus_z = 0.5 * (centre + padded[:-2, 1:-1, 1:-1])
    plus_z = 0.5 * (centre + padded[2:, 1:-1, 1:-1])
    minus_x = 0.5 * (centre + padded[1:-1, :-2, 1:-1])
    plus_x = 0.5 * (centre + padded[1:-1, 2:, 1:-1])
    minus_y = 0.5 * (centre + padded[1:-1, 1:-1, :-2])
    plus_y = 0.5 * (centre + padded[1:-1, 1:-1, 2:])
    diagonal = ((((minus_z + plus_z) + minus_x) + plus_x) + minus_y) + plus_y
    return (minus_z, plus_z, minus_x, plus_x, minus_y, plus_y, diagonal)


def pull(field_edged, coefs):
    padded = jnp.pad(field_edged, ((1, 1), (0, 0), (0, 0)))
    total = coefs[0] * padded[:-2, 1:-1, 1:-1]
    total = total + coefs[1] * padded[2:, 1:-1, 1:-1]
    total = total + coefs[2] * padded[1:-1, :-2, 1:-1]
    total = total + coefs[3] * padded[1:-1, 2:, 1:-1]
    total = total + coefs[4] * padded[1:-1, 1:-1, :-2]
    total = total + coefs[5] * padded[1:-1, 1:-1, 2:]
    return total


def relax(field_edged, rhs_part, coefs, colour_mask):
    centre = field_edged[:, 1:-1, 1:-1]
    updated = (rhs_part + pull(field_edged, coefs)) / coefs[6]
    return jnp.where(colour_mask, updated, centre)


def parity(shape, colour):
    depth = lax.broadcasted_iota(jnp.int32, shape, 0)
    across = lax.broadcasted_iota(jnp.int32, shape, 1)
    along = lax.broadcasted_iota(jnp.int32, shape, 2)
    return ((depth + across + along) % 2) == colour


def reference(source, coefficient, initial_guess, box_place):
    rhs_grid = to_grid(source, box_place)
    beta_grid = to_grid(coefficient, box_place)
    solution = to_grid(initial_guess, box_place)
    coefs = face_terms(pad_plane(beta_grid))
    masks = (parity(rhs_grid.shape, 0), parity(rhs_grid.shape, 1))
    for sweep_index in range(SWEEPS):
        for colour in range(2):
            solution = relax(pad_plane(solution), rhs_grid, coefs, masks[colour])
    residual = rhs_grid - (coefs[6] * solution - pull(pad_plane(solution), coefs))
    return solution, residual
```

```python
import jax
import jax.numpy as jnp
from jax import lax
from jax.experimental import pallas as pl
from jax.experimental.pallas import tpu as pltpu
from jax.sharding import PartitionSpec as P

MESH = pl.DeviceIdType.MESH
F32 = jnp.float32
NX = 8
NY = 16
ND = NX * NY
BZ = 4
LANES = 128
ROWS = 72
COLS = 640
OWN_TILES = 8
TILES = ROWS // 8
SWEEPS = 2
STRIDE = 37

BETA_K, BETA_R, PHI_K, RHS_R, RHS_K = range(5)
FIELDS = ((0, 2), (2, 1), (3, 2))


def invert_kernel(place_ref, out_ref):
    place = place_ref[...]
    boxes = place.shape[1]
    box = lax.broadcasted_iota(jnp.int32, (NX * 2, boxes), 1)
    high = lax.broadcasted_iota(jnp.int32, (NX * 2, boxes), 0) == place // LANES
    low = lax.broadcasted_iota(jnp.int32, (LANES, boxes), 0) == place % LANES
    low = jnp.where(low, 1.0, 0.0).astype(jnp.bfloat16)
    dims = (((1,), (1,)), ((), ()))
    tops = jnp.where(high, box // 16, 0).astype(F32).astype(jnp.bfloat16)
    ends = jnp.where(high, box % 16, 0).astype(F32).astype(jnp.bfloat16)
    tops = lax.dot_general(tops, low, dims, preferred_element_type=F32)
    ends = lax.dot_general(ends, low, dims, preferred_element_type=F32)
    out_ref[...] = (tops * 16.0 + ends).astype(jnp.int32)


def kernel(
    src, coef, guess, inv, sol, res,
    stage, s1b, s1g, s1r, g1b, g1g, g1r, dup, s2b, s2g, s2r, g2b, g2g, g2r,
    ext, red, faces, diag, inverse, black_res, parts, ysend, yrecv, xrecv,
    in_sem, s1_sem, r1_sem, s2_sem, r2_sem, ys_sem, yr_sem, xs_sem, xr_sem, out_sem,
):
    i = lax.axis_index("bx")
    j = lax.axis_index("by")
    me = i * NY + j
    s1, g1 = (s1b, s1g, s1r), (g1b, g1g, g1r)
    s2, g2 = (s2b, s2g, s2r), (g2b, g2g, g2r)
    depth = (16, 8, 16)
    lane = lax.broadcasted_iota(jnp.int32, (8, LANES), 1)
    low = lane < 64

    loads = [
        pltpu.make_async_copy(ref, stage.at[f], in_sem.at[f])
        for f, ref in enumerate((coef, guess, src))
    ]
    for load in loads:
        load.start()

    barrier = pltpu.get_barrier_semaphore()

    def greet(s, _):
        t = lax.rem(me + s, ND)
        pl.semaphore_signal(barrier, inc=1, device_id=(t // NY, lax.rem(t, NY)), device_id_type=MESH)
        return 0

    lax.fori_loop(1, ND, greet, 0)

    def packed(f, q):
        cols = pl.ds(pl.multiple_of(q * LANES, LANES), LANES)
        first, second = stage[f, 0:8, cols], stage[f, 8:16, cols]
        even = jnp.where(low, first, pltpu.roll(second, 64, 1))
        odd = jnp.where(low, pltpu.roll(first, 64, 1), second)
        mask = (lane + q // 32) % 2 == 0
        return jnp.where(mask, even, odd), jnp.where(mask, odd, even)

    def pack_beta(q, _):
        r, k = packed(0, q)
        s1b[q, 0:8, :] = k
        s1b[q, 8:16, :] = r
        return 0

    def pack_guess(q, _):
        s1g[q, :, :] = packed(1, q)[1]
        return 0

    def pack_rhs(q, _):
        r, k = packed(2, q)
        s1r[q, 0:8, :] = r
        s1r[q, 8:16, :] = k
        return 0

    for f, pack in enumerate((pack_beta, pack_guess, pack_rhs)):
        loads[f].wait()
        lax.fori_loop(0, ND, pack, 0)

    pl.semaphore_wait(barrier, ND - 1)

    for f in range(3):
        def spread(s, _, f=f):
            t = lax.rem(me + s * STRIDE, ND)
            pltpu.make_async_remote_copy(
                s1[f].at[t], g1[f].at[me], s1_sem.at[f], r1_sem.at[f],
                device_id=(t // NY, lax.rem(t, NY)), device_id_type=MESH,
            ).start()
            return 0

        pltpu.make_async_copy(s1[f].at[me], g1[f].at[me], r1_sem.at[f]).start()
        lax.fori_loop(1, ND, spread, 0)

    low_row = lax.broadcasted_iota(jnp.int32, (1, LANES), 1) < 64
    for f in range(3):
        planes = depth[f] // 8
        pltpu.make_async_copy(g1[f], g1[f], r1_sem.at[f]).wait()

        def double(d, _, f=f, planes=planes):
            for p in range(planes):
                rows = g1[f][d, p * 8 : p * 8 + 8, :]
                other = pltpu.roll(rows, 64, 1)
                at = pl.multiple_of(d * 16, 16)
                dup[p, pl.ds(at, 8), :] = jnp.where(low, rows, other)
                dup[p, pl.ds(at + 8, 8), :] = jnp.where(low, other, rows)
            return 0

        lax.fori_loop(0, ND, double, 0)

        def gather(t, f=f, planes=planes):
            ti, tj = t // NY, lax.rem(t, NY)
            for tx in range(2):
                for m in range(4):
                    a = inv[ti * 2 + tx, tj * 8 + 2 * m]
                    b = inv[ti * 2 + tx, tj * 8 + 2 * m + 1]
                    for p in range(planes):
                        row = jnp.where(low_row, dup[p, pl.ds(a, 1), :], dup[p, pl.ds(b, 1), :])
                        s2[f][t, pl.ds(p * 8 + tx * 4 + m, 1), :] = row

        gather(me)
        pltpu.make_async_copy(s2[f].at[me], g2[f].at[pl.ds(me * depth[f], depth[f])], r2_sem.at[f]).start()

        def place(s, _, f=f, gather=gather):
            t = lax.rem(me + s * STRIDE, ND)
            gather(t)
            pltpu.make_async_remote_copy(
                s2[f].at[t], g2[f].at[pl.ds(me * depth[f], depth[f])], s2_sem.at[f], r2_sem.at[f],
                device_id=(t // NY, lax.rem(t, NY)), device_id_type=MESH,
            ).start()
            return 0

        lax.fori_loop(1, ND, place, 0)

    left = (i, lax.rem(j + NY - 1, NY))
    right = (i, lax.rem(j + 1, NY))
    above = (lax.rem(i + NX - 1, NX), j)
    below = (lax.rem(i + 1, NX), j)

    def y_copies(f):
        first, count = FIELDS[f]
        return [
            pltpu.make_async_remote_copy(
                ysend.at[pl.ds(first, count), side], yrecv.at[pl.ds(first, count), side],
                ys_sem.at[f, side], yr_sem.at[f, side], device_id=device, device_id_type=MESH,
            )
            for side, device in enumerate((left, right))
        ]

    def x_copies(f):
        first, count = FIELDS[f]
        return [
            pltpu.make_async_remote_copy(
                ext.at[pl.ds(first, count), :, pl.ds(start, 8), :], xrecv.at[pl.ds(first, count), side],
                xs_sem.at[f, side], xr_sem.at[f, side], device_id=device, device_id_type=MESH,
            )
            for side, (start, device) in enumerate(((0, above), (56, below)))
        ]

    def lay_out(f):
        pltpu.make_async_copy(g2[f], g2[f], r2_sem.at[f]).wait()
        first, count = FIELDS[f]
        for p in range(count):
            for z in range(BZ):
                for tile in range(OWN_TILES):
                    start = (z * 32 + tile % 4 * 8) * depth[f] + p * 8 + tile // 4 * 4
                    for m in range(4):
                        ext[first + p, z, tile * 8 : tile * 8 + 8, m * LANES : (m + 1) * LANES] = g2[f][
                            pl.ds(start + m, 8, stride=depth[f]), :
                        ]
            for g in range(2):
                to_left = jnp.zeros((8, LANES), F32)
                to_right = jnp.zeros((8, LANES), F32)
                for c in range(16):
                    z, tile = divmod(g * 16 + c, OWN_TILES)
                    rows = slice(tile * 8, tile * 8 + 8)
                    mask = lane // 8 == c
                    head = ext[first + p, z, rows, 0:LANES]
                    tail = ext[first + p, z, rows, 3 * LANES : 4 * LANES]
                    to_left = jnp.where(mask, pltpu.roll(head, 8 * c, 1), to_left)
                    to_right = jnp.where(mask, pltpu.roll(tail, (8 * c + 8) % LANES, 1), to_right)
                ysend[first + p, 0, g] = to_left
                ysend[first + p, 1, g] = to_right
        for copy in y_copies(f):
            copy.start()

    from_right = (lane < 8) & (j < NY - 1)
    from_left = (lane >= 120) & (j > 0)

    def merge_y(f):
        first, count = FIELDS[f]
        for copy in y_copies(f):
            copy.wait_recv()
        for p in range(first, first + count):
            for n in range(BZ * OWN_TILES):
                g, c = divmod(n, 16)
                z, tile = divmod(n, OWN_TILES)
                head = pltpu.roll(yrecv[p, 0, g], (LANES - 8 * c) % LANES, 1)
                tail = pltpu.roll(yrecv[p, 1, g], 120 - 8 * c, 1)
                ext[p, z, tile * 8 : tile * 8 + 8, 4 * LANES :] = jnp.where(
                    from_right, head, jnp.where(from_left, tail, 0.0)
                )
        for copy in x_copies(f):
            copy.start()

    row = lax.broadcasted_iota(jnp.int32, (8, COLS), 0)
    from_below = (row < 4) & (i < NX - 1)
    from_above = (row >= 4) & (i > 0)

    def merge_x(f):
        first, count = FIELDS[f]
        for copy in x_copies(f):
            copy.wait_recv()
        for p in range(first, first + count):
            for z in range(BZ):
                ext[p, z, 64:72, :] = jnp.where(
                    from_below, xrecv[p, 0, z], jnp.where(from_above, xrecv[p, 1, z], 0.0)
                )

    column = lax.broadcasted_iota(jnp.int32, (8, COLS), 1)

    def tile_rows(tile):
        return pl.ds(pl.multiple_of(tile * 8, 8), 8)

    def neighbours(ref, colour, z, tile):
        here = tile_rows(tile)
        current = ref[z, here, :]
        before = ref[z, tile_rows(lax.rem(tile + TILES - 1, TILES)), :]
        after = ref[z, tile_rows(lax.rem(tile + 1, TILES)), :]
        minus = jnp.where(row == 0, pltpu.roll(before, 1, 0), pltpu.roll(current, 1, 0))
        plus = jnp.where(row == 7, pltpu.roll(after, 7, 0), pltpu.roll(current, 7, 0))
        even_x = (column + z) % 2 == colour
        return (
            ref[z - 1, here, :] if z > 0 else None,
            ref[z + 1, here, :] if z < BZ - 1 else None,
            current,
            jnp.where(even_x, minus, plus),
            pltpu.roll(current, 1, 1),
            pltpu.roll(current, COLS - 1, 1),
        )

    def make_faces(tile, _):
        here = tile_rows(tile)
        for colour in range(2):
            centre_ref, other_ref = (ext.at[BETA_R], ext.at[BETA_K]) if colour == 0 else (ext.at[BETA_K], ext.at[BETA_R])
            for z in range(BZ):
                centre = centre_ref[z, here, :]
                total = None
                for n, value in enumerate(neighbours(other_ref, colour, z, tile)):
                    face = 0.5 * centre if value is None else 0.5 * (centre + value)
                    if value is not None:
                        faces[colour, n, z, here, :] = face
                    total = face if total is None else total + face
                inside = centre > 0.0
                diag[colour, z, here, :] = total
                inverse[colour, z, here, :] = jnp.where(inside, 1.0 / jnp.where(inside, total, 1.0), 0.0)
        return 0

    def pulled(colour, other_ref, rhs_plane, z, tile):
        here = tile_rows(tile)
        total = ext[rhs_plane, z, here, :]
        for n, value in enumerate(neighbours(other_ref, colour, z, tile)):
            if value is not None:
                total = total + faces[colour, n, z, here, :] * value
        return total

    def update_red(tile, _):
        here = tile_rows(tile)
        for z in range(BZ):
            red[z, here, :] = pulled(0, ext.at[PHI_K], RHS_R, z, tile) * inverse[0, z, here, :]
        return 0

    def update_black(tile, _):
        here = tile_rows(tile)
        for z in range(BZ):
            ext[PHI_K, z, here, :] = pulled(1, red, RHS_K, z, tile) * inverse[1, z, here, :]
        return 0

    own = 4 * LANES

    def write(out, z, tile, red_part, black_part):
        even_x = (column[:, :own] + z) % 2 == 0
        start = pl.multiple_of(tile * 16, 16)
        even, odd = jnp.where(even_x, red_part, black_part), jnp.where(even_x, black_part, red_part)
        for m in range(4):
            part = slice(m * LANES, (m + 1) * LANES)
            parts[out, z, m, pl.ds(start, 8, stride=2), :] = even[:, part]
            parts[out, z, m, pl.ds(start + 1, 8, stride=2), :] = odd[:, part]

    def last_black(tile, _):
        here = tile_rows(tile)
        for z in range(BZ):
            total = pulled(1, red, RHS_K, z, tile)
            value = total * inverse[1, z, here, :]
            ext[PHI_K, z, here, :] = value
            black_res[z, here, :] = total - diag[1, z, here, :] * value
        return 0

    def outputs(tile, _):
        here = tile_rows(tile)
        for z in range(BZ):
            red_value = red[z, here, :]
            total = pulled(0, ext.at[PHI_K], RHS_R, z, tile)
            red_res = total - diag[0, z, here, :] * red_value
            write(0, z, tile, red_value[:, :own], ext[PHI_K, z, here, :][:, :own])
            write(1, z, tile, red_res[:, :own], black_res[z, here, :][:, :own])
        rows = pl.ds(pl.multiple_of(tile * 16, 16), 16)
        for n, out in enumerate((sol, res)):
            for m in range(4):
                pltpu.make_async_copy(
                    parts.at[n, :, m, rows, :], out.at[:, rows, pl.ds(m * LANES, LANES)], out_sem.at[n]
                ).start()
        return 0

    lay_out(0)
    lay_out(1)
    merge_y(0)
    merge_y(1)
    merge_x(0)
    merge_x(1)
    lax.fori_loop(0, TILES, make_faces, 0)
    lay_out(2)
    merge_y(2)
    merge_x(2)
    for copy in x_copies(1):
        copy.wait_send()
    for sweep in range(SWEEPS):
        lax.fori_loop(0, TILES, update_red, 0)
        lax.fori_loop(0, TILES, update_black if sweep < SWEEPS - 1 else last_black, 0)
    lax.fori_loop(0, OWN_TILES, outputs, 0)

    for n, out in enumerate((sol, res)):
        pltpu.make_async_copy(out, out, out_sem.at[n]).wait()
    for f in range(3):
        part = s1[f].at[pl.ds(0, ND - 1)]
        pltpu.make_async_copy(part, part, s1_sem.at[f]).wait()
        pltpu.make_async_copy(part, part, s2_sem.at[f]).wait()
        for copy in y_copies(f):
            copy.wait_send()
    for f in (0, 2):
        for copy in x_copies(f):
            copy.wait_send()


def local(source, coefficient, initial_guess, box_place):
    inverse_place = pl.pallas_call(
        invert_kernel,
        out_shape=jax.ShapeDtypeStruct((NX * 2, LANES), jnp.int32),
        in_specs=[pl.BlockSpec(memory_space=pltpu.VMEM)],
        out_specs=pl.BlockSpec(memory_space=pltpu.VMEM),
    )(box_place.reshape(1, -1))
    tile = (BZ, 128, 512)
    vmem, dma = pltpu.VMEM, pltpu.SemaphoreType.DMA
    plane = (BZ, ROWS, COLS)
    any_spec = pl.BlockSpec(memory_space=pl.ANY)
    return pl.pallas_call(
        kernel,
        out_shape=(jax.ShapeDtypeStruct(tile, F32),) * 2,
        in_specs=[any_spec] * 3 + [pl.BlockSpec(memory_space=pltpu.SMEM)],
        out_specs=(any_spec,) * 2,
        scratch_shapes=[
            vmem((3, 16, 16384), F32),
            *[vmem((ND, rows, LANES), F32) for rows in (16, 8, 16)],
            *[vmem((ND, rows, LANES), F32) for rows in (16, 8, 16)],
            vmem((2, ND * 16, LANES), F32),
            *[vmem((ND, rows, LANES), F32) for rows in (16, 8, 16)],
            *[vmem((ND * rows, LANES), F32) for rows in (16, 8, 16)],
            vmem((5, *plane), F32),
            vmem(plane, F32),
            vmem((2, 6, *plane), F32),
            vmem((2, *plane), F32),
            vmem((2, *plane), F32),
            vmem(plane, F32),
            vmem((2, BZ, 4, 128, LANES), F32),
            vmem((5, 2, 2, 8, LANES), F32),
            vmem((5, 2, 2, 8, LANES), F32),
            vmem((5, 2, BZ, 8, COLS), F32),
            dma((3,)),
            dma((3,)),
            dma((3,)),
            dma((3,)),
            dma((3,)),
            dma((3, 2)),
            dma((3, 2)),
            dma((3, 2)),
            dma((3, 2)),
            dma((2,)),
        ],
        compiler_params=pltpu.CompilerParams(
            collective_id=0, has_side_effects=True, vmem_limit_bytes=48 << 20
        ),
    )(source, coefficient, initial_guess, inverse_place)


def solution(mesh):
    boxes = P(("bx", "by"), None)
    out = P(None, "bx", "by")
    return jax.shard_map(
        local,
        mesh=mesh,
        in_specs=(boxes, boxes, boxes, P()),
        out_specs=(out, out),
        check_vma=False,
    )
```

```python
import jax
import jax.numpy as jnp
from jax import lax
from jax.experimental import pallas as pl
from jax.experimental.pallas import tpu as pltpu
from jax.sharding import PartitionSpec as P

MESH = pl.DeviceIdType.MESH
F32 = jnp.float32
NX = 8
NY = 16
ND = NX * NY
BZ = 4
LANES = 128
ROWS = 72
COLS = 640
OWN_TILES = 8
TILES = ROWS // 8
SWEEPS = 2
STRIDE = 37
GROUP = 8

BETA_K, BETA_R, PHI_K, RHS_R, RHS_K = range(5)
FIELDS = ((0, 2), (2, 1), (3, 2))


def invert_kernel(place_ref, out_ref):
    place = place_ref[...]
    boxes = place.shape[1]
    box = lax.broadcasted_iota(jnp.int32, (NX * 2, boxes), 1)
    high = lax.broadcasted_iota(jnp.int32, (NX * 2, boxes), 0) == place // LANES
    low = lax.broadcasted_iota(jnp.int32, (LANES, boxes), 0) == place % LANES
    low = jnp.where(low, 1.0, 0.0).astype(jnp.bfloat16)
    dims = (((1,), (1,)), ((), ()))
    tops = jnp.where(high, box // 16, 0).astype(F32).astype(jnp.bfloat16)
    ends = jnp.where(high, box % 16, 0).astype(F32).astype(jnp.bfloat16)
    tops = lax.dot_general(tops, low, dims, preferred_element_type=F32)
    ends = lax.dot_general(ends, low, dims, preferred_element_type=F32)
    out_ref[...] = (tops * 16.0 + ends).astype(jnp.int32)


def kernel(
    src, coef, guess, inv, sol, res,
    stage, s1b, s1g, s1r, g1b, g1g, g1r, dup, s2b, s2g, s2r, g2b, g2g, g2r,
    ext, red, faces, diag, inverse, black_res, parts, ysend, yrecv, xrecv,
    in_sem, s1_sem, r1_sem, s2_sem, r2_sem, ys_sem, yr_sem, xs_sem, xr_sem, out_sem,
):
    i = lax.axis_index("bx")
    j = lax.axis_index("by")
    me = i * NY + j
    s1, g1 = (s1b, s1g, s1r), (g1b, g1g, g1r)
    s2, g2 = (s2b, s2g, s2r), (g2b, g2g, g2r)
    depth = (16, 8, 16)
    lane = lax.broadcasted_iota(jnp.int32, (8, LANES), 1)
    low = lane < 64

    loads = [
        pltpu.make_async_copy(ref, stage.at[f], in_sem.at[f])
        for f, ref in enumerate((coef, guess, src))
    ]
    for load in loads:
        load.start()

    barrier = pltpu.get_barrier_semaphore()

    def greet(s, _):
        t = lax.rem(me + s, ND)
        pl.semaphore_signal(barrier, inc=1, device_id=(t // NY, lax.rem(t, NY)), device_id_type=MESH)
        return 0

    lax.fori_loop(1, ND, greet, 0)

    def packed(f, q):
        cols = pl.ds(pl.multiple_of(q * LANES, LANES), LANES)
        first, second = stage[f, 0:8, cols], stage[f, 8:16, cols]
        even = jnp.where(low, first, pltpu.roll(second, 64, 1))
        odd = jnp.where(low, pltpu.roll(first, 64, 1), second)
        mask = (lane + q // 32) % 2 == 0
        return jnp.where(mask, even, odd), jnp.where(mask, odd, even)

    def pack_beta(q, _):
        r, k = packed(0, q)
        s1b[q, 0:8, :] = k
        s1b[q, 8:16, :] = r
        return 0

    def pack_guess(q, _):
        s1g[q, :, :] = packed(1, q)[1]
        return 0

    def pack_rhs(q, _):
        r, k = packed(2, q)
        s1r[q, 0:8, :] = r
        s1r[q, 8:16, :] = k
        return 0

    for f, pack in enumerate((pack_beta, pack_guess, pack_rhs)):
        loads[f].wait()
        lax.fori_loop(0, ND, pack, 0, unroll=8)

    pl.semaphore_wait(barrier, ND - 1)

    for f in range(3):
        def spread(s, _, f=f):
            t = lax.rem(me + s * STRIDE, ND)
            pltpu.make_async_remote_copy(
                s1[f].at[t], g1[f].at[me], s1_sem.at[f], r1_sem.at[f],
                device_id=(t // NY, lax.rem(t, NY)), device_id_type=MESH,
            ).start()
            return 0

        pltpu.make_async_copy(s1[f].at[me], g1[f].at[me], r1_sem.at[f]).start()
        lax.fori_loop(1, ND, spread, 0)

    low_row = lax.broadcasted_iota(jnp.int32, (1, LANES), 1) < 64
    for f in range(3):
        planes = depth[f] // 8
        pltpu.make_async_copy(g1[f], g1[f], r1_sem.at[f]).wait()

        def double(d, _, f=f, planes=planes):
            for p in range(planes):
                rows = g1[f][d, p * 8 : p * 8 + 8, :]
                other = pltpu.roll(rows, 64, 1)
                at = pl.multiple_of(d * 16, 16)
                dup[p, pl.ds(at, 8), :] = jnp.where(low, rows, other)
                dup[p, pl.ds(at + 8, 8), :] = jnp.where(low, other, rows)
            return 0

        lax.fori_loop(0, ND, double, 0, unroll=8)

        def gather(t, f=f, planes=planes):
            ti, tj = t // NY, lax.rem(t, NY)
            for tx in range(2):
                for m in range(4):
                    a = inv[ti * 2 + tx, tj * 8 + 2 * m]
                    b = inv[ti * 2 + tx, tj * 8 + 2 * m + 1]
                    for p in range(planes):
                        row = jnp.where(low_row, dup[p, pl.ds(a, 1), :], dup[p, pl.ds(b, 1), :])
                        s2[f][t, pl.ds(p * 8 + tx * 4 + m, 1), :] = row

        def send(t, f=f):
            pltpu.make_async_remote_copy(
                s2[f].at[t], g2[f].at[pl.ds(me * depth[f], depth[f])], s2_sem.at[f], r2_sem.at[f],
                device_id=(t // NY, lax.rem(t, NY)), device_id_type=MESH,
            ).start()

        def group(first, count, gather=gather, send=send):
            tiles = [lax.rem(me + (first + n) * STRIDE, ND) for n in range(count)]
            for t in tiles:
                gather(t)
            for t in tiles:
                send(t)

        def place(n, _, group=group):
            group(1 + n * GROUP, GROUP)
            return 0

        lax.fori_loop(0, (ND - 1) // GROUP, place, 0)
        group(1 + (ND - 1) // GROUP * GROUP, (ND - 1) % GROUP)
        gather(me)
        pltpu.make_async_copy(s2[f].at[me], g2[f].at[pl.ds(me * depth[f], depth[f])], r2_sem.at[f]).start()

    left = (i, lax.rem(j + NY - 1, NY))
    right = (i, lax.rem(j + 1, NY))
    above = (lax.rem(i + NX - 1, NX), j)
    below = (lax.rem(i + 1, NX), j)

    def y_copies(f):
        first, count = FIELDS[f]
        return [
            pltpu.make_async_remote_copy(
                ysend.at[pl.ds(first, count), side], yrecv.at[pl.ds(first, count), side],
                ys_sem.at[f, side], yr_sem.at[f, side], device_id=device, device_id_type=MESH,
            )
            for side, device in enumerate((left, right))
        ]

    def x_copies(f):
        first, count = FIELDS[f]
        return [
            pltpu.make_async_remote_copy(
                ext.at[pl.ds(first, count), :, pl.ds(start, 8), :], xrecv.at[pl.ds(first, count), side],
                xs_sem.at[f, side], xr_sem.at[f, side], device_id=device, device_id_type=MESH,
            )
            for side, (start, device) in enumerate(((0, above), (56, below)))
        ]

    def lay_out(f):
        pltpu.make_async_copy(g2[f], g2[f], r2_sem.at[f]).wait()
        first, count = FIELDS[f]
        for p in range(count):
            for z in range(BZ):
                for tile in range(OWN_TILES):
                    start = (z * 32 + tile % 4 * 8) * depth[f] + p * 8 + tile // 4 * 4
                    for m in range(4):
                        ext[first + p, z, tile * 8 : tile * 8 + 8, m * LANES : (m + 1) * LANES] = g2[f][
                            pl.ds(start + m, 8, stride=depth[f]), :
                        ]
            for g in range(2):
                to_left = jnp.zeros((8, LANES), F32)
                to_right = jnp.zeros((8, LANES), F32)
                for c in range(16):
                    z, tile = divmod(g * 16 + c, OWN_TILES)
                    rows = slice(tile * 8, tile * 8 + 8)
                    mask = lane // 8 == c
                    head = ext[first + p, z, rows, 0:LANES]
                    tail = ext[first + p, z, rows, 3 * LANES : 4 * LANES]
                    to_left = jnp.where(mask, pltpu.roll(head, 8 * c, 1), to_left)
                    to_right = jnp.where(mask, pltpu.roll(tail, (8 * c + 8) % LANES, 1), to_right)
                ysend[first + p, 0, g] = to_left
                ysend[first + p, 1, g] = to_right
        for copy in y_copies(f):
            copy.start()

    from_right = (lane < 8) & (j < NY - 1)
    from_left = (lane >= 120) & (j > 0)

    def merge_y(f):
        first, count = FIELDS[f]
        for copy in y_copies(f):
            copy.wait_recv()
        for p in range(first, first + count):
            for n in range(BZ * OWN_TILES):
                g, c = divmod(n, 16)
                z, tile = divmod(n, OWN_TILES)
                head = pltpu.roll(yrecv[p, 0, g], (LANES - 8 * c) % LANES, 1)
                tail = pltpu.roll(yrecv[p, 1, g], 120 - 8 * c, 1)
                ext[p, z, tile * 8 : tile * 8 + 8, 4 * LANES :] = jnp.where(
                    from_right, head, jnp.where(from_left, tail, 0.0)
                )
        for copy in x_copies(f):
            copy.start()

    row = lax.broadcasted_iota(jnp.int32, (8, COLS), 0)
    from_below = (row < 4) & (i < NX - 1)
    from_above = (row >= 4) & (i > 0)

    def merge_x(f):
        first, count = FIELDS[f]
        for copy in x_copies(f):
            copy.wait_recv()
        for p in range(first, first + count):
            for z in range(BZ):
                ext[p, z, 64:72, :] = jnp.where(
                    from_below, xrecv[p, 0, z], jnp.where(from_above, xrecv[p, 1, z], 0.0)
                )

    column = lax.broadcasted_iota(jnp.int32, (8, COLS), 1)

    def tile_rows(tile):
        return pl.ds(pl.multiple_of(tile * 8, 8), 8)

    def neighbours(ref, colour, z, tile):
        here = tile_rows(tile)
        current = ref[z, here, :]
        before = ref[z, tile_rows(lax.rem(tile + TILES - 1, TILES)), :]
        after = ref[z, tile_rows(lax.rem(tile + 1, TILES)), :]
        minus = jnp.where(row == 0, pltpu.roll(before, 1, 0), pltpu.roll(current, 1, 0))
        plus = jnp.where(row == 7, pltpu.roll(after, 7, 0), pltpu.roll(current, 7, 0))
        even_x = (column + z) % 2 == colour
        return (
            ref[z - 1, here, :] if z > 0 else None,
            ref[z + 1, here, :] if z < BZ - 1 else None,
            current,
            jnp.where(even_x, minus, plus),
            pltpu.roll(current, 1, 1),
            pltpu.roll(current, COLS - 1, 1),
        )

    def make_faces(tile, _):
        here = tile_rows(tile)
        for colour in range(2):
            centre_ref, other_ref = (ext.at[BETA_R], ext.at[BETA_K]) if colour == 0 else (ext.at[BETA_K], ext.at[BETA_R])
            for z in range(BZ):
                centre = centre_ref[z, here, :]
                total = None
                for n, value in enumerate(neighbours(other_ref, colour, z, tile)):
                    face = 0.5 * centre if value is None else 0.5 * (centre + value)
                    if value is not None:
                        faces[colour, n, z, here, :] = face
                    total = face if total is None else total + face
                inside = centre > 0.0
                diag[colour, z, here, :] = total
                inverse[colour, z, here, :] = jnp.where(inside, 1.0 / jnp.where(inside, total, 1.0), 0.0)
        return 0

    def pulled(colour, other_ref, rhs_plane, z, tile):
        here = tile_rows(tile)
        total = ext[rhs_plane, z, here, :]
        for n, value in enumerate(neighbours(other_ref, colour, z, tile)):
            if value is not None:
                total = total + faces[colour, n, z, here, :] * value
        return total

    def update_red(tile, _):
        here = tile_rows(tile)
        for z in range(BZ):
            red[z, here, :] = pulled(0, ext.at[PHI_K], RHS_R, z, tile) * inverse[0, z, here, :]
        return 0

    def update_black(tile, _):
        here = tile_rows(tile)
        for z in range(BZ):
            ext[PHI_K, z, here, :] = pulled(1, red, RHS_K, z, tile) * inverse[1, z, here, :]
        return 0

    own = 4 * LANES

    def write(out, z, tile, red_part, black_part):
        even_x = (column[:, :own] + z) % 2 == 0
        start = pl.multiple_of(tile * 16, 16)
        even, odd = jnp.where(even_x, red_part, black_part), jnp.where(even_x, black_part, red_part)
        for m in range(4):
            part = slice(m * LANES, (m + 1) * LANES)
            parts[out, z, m, pl.ds(start, 8, stride=2), :] = even[:, part]
            parts[out, z, m, pl.ds(start + 1, 8, stride=2), :] = odd[:, part]

    def last_black(tile, _):
        here = tile_rows(tile)
        for z in range(BZ):
            total = pulled(1, red, RHS_K, z, tile)
            value = total * inverse[1, z, here, :]
            ext[PHI_K, z, here, :] = value
            black_res[z, here, :] = total - diag[1, z, here, :] * value
        return 0

    def outputs(tile, _):
        here = tile_rows(tile)
        for z in range(BZ):
            red_value = red[z, here, :]
            total = pulled(0, ext.at[PHI_K], RHS_R, z, tile)
            red_res = total - diag[0, z, here, :] * red_value
            write(0, z, tile, red_value[:, :own], ext[PHI_K, z, here, :][:, :own])
            write(1, z, tile, red_res[:, :own], black_res[z, here, :][:, :own])
        rows = pl.ds(pl.multiple_of(tile * 16, 16), 16)
        for n, out in enumerate((sol, res)):
            for m in range(4):
                pltpu.make_async_copy(
                    parts.at[n, :, m, rows, :], out.at[:, rows, pl.ds(m * LANES, LANES)], out_sem.at[n]
                ).start()
        return 0

    lay_out(0)
    lay_out(1)
    merge_y(0)
    merge_y(1)
    merge_x(0)
    merge_x(1)
    lax.fori_loop(0, TILES, make_faces, 0)
    lay_out(2)
    merge_y(2)
    merge_x(2)
    for copy in x_copies(1):
        copy.wait_send()
    for sweep in range(SWEEPS):
        lax.fori_loop(0, TILES, update_red, 0)
        lax.fori_loop(0, TILES, update_black if sweep < SWEEPS - 1 else last_black, 0)
    lax.fori_loop(0, OWN_TILES, outputs, 0)

    for n, out in enumerate((sol, res)):
        pltpu.make_async_copy(out, out, out_sem.at[n]).wait()
    for f in range(3):
        part = s1[f].at[pl.ds(0, ND - 1)]
        pltpu.make_async_copy(part, part, s1_sem.at[f]).wait()
        pltpu.make_async_copy(part, part, s2_sem.at[f]).wait()
        for copy in y_copies(f):
            copy.wait_send()
    for f in (0, 2):
        for copy in x_copies(f):
            copy.wait_send()


def local(source, coefficient, initial_guess, box_place):
    inverse_place = pl.pallas_call(
        invert_kernel,
        out_shape=jax.ShapeDtypeStruct((NX * 2, LANES), jnp.int32),
        in_specs=[pl.BlockSpec(memory_space=pltpu.VMEM)],
        out_specs=pl.BlockSpec(memory_space=pltpu.VMEM),
    )(box_place.reshape(1, -1))
    tile = (BZ, 128, 512)
    vmem, dma = pltpu.VMEM, pltpu.SemaphoreType.DMA
    plane = (BZ, ROWS, COLS)
    any_spec = pl.BlockSpec(memory_space=pl.ANY)
    return pl.pallas_call(
        kernel,
        out_shape=(jax.ShapeDtypeStruct(tile, F32),) * 2,
        in_specs=[any_spec] * 3 + [pl.BlockSpec(memory_space=pltpu.SMEM)],
        out_specs=(any_spec,) * 2,
        scratch_shapes=[
            vmem((3, 16, 16384), F32),
            *[vmem((ND, rows, LANES), F32) for rows in (16, 8, 16)],
            *[vmem((ND, rows, LANES), F32) for rows in (16, 8, 16)],
            vmem((2, ND * 16, LANES), F32),
            *[vmem((ND, rows, LANES), F32) for rows in (16, 8, 16)],
            *[vmem((ND * rows, LANES), F32) for rows in (16, 8, 16)],
            vmem((5, *plane), F32),
            vmem(plane, F32),
            vmem((2, 6, *plane), F32),
            vmem((2, *plane), F32),
            vmem((2, *plane), F32),
            vmem(plane, F32),
            vmem((2, BZ, 4, 128, LANES), F32),
            vmem((5, 2, 2, 8, LANES), F32),
            vmem((5, 2, 2, 8, LANES), F32),
            vmem((5, 2, BZ, 8, COLS), F32),
            dma((3,)),
            dma((3,)),
            dma((3,)),
            dma((3,)),
            dma((3,)),
            dma((3, 2)),
            dma((3, 2)),
            dma((3, 2)),
            dma((3, 2)),
            dma((2,)),
        ],
        compiler_params=pltpu.CompilerParams(
            collective_id=0, has_side_effects=True, vmem_limit_bytes=60 << 20
        ),
    )(source, coefficient, initial_guess, inverse_place)


def solution(mesh):
    boxes = P(("bx", "by"), None)
    out = P(None, "bx", "by")
    return jax.shard_map(
        local,
        mesh=mesh,
        in_specs=(boxes, boxes, boxes, P()),
        out_specs=(out, out),
        check_vma=False,
    )
```

```python
import jax
import jax.numpy as jnp
from jax import lax
from jax.experimental import pallas as pl
from jax.experimental.pallas import tpu as pltpu
from jax.sharding import PartitionSpec as P

MESH = pl.DeviceIdType.MESH
F32 = jnp.float32
NX = 8
NY = 16
ND = NX * NY
BZ = 4
LANES = 128
ROWS = 72
COLS = 640
OWN_TILES = 8
TILES = ROWS // 8
SWEEPS = 2
STRIDE = 37
GROUP = 8

BETA_K, BETA_R, PHI_K, RHS_R, RHS_K = range(5)
UNITS = ((0, 2, 0), (2, 1, 1), (3, 1, 2), (4, 1, 2))


def store_kernel(parts, sol, res, sems):
    for n, out in enumerate((sol, res)):
        for m in range(4):
            pltpu.make_async_copy(parts.at[n, :, m], out.at[:, :, pl.ds(m * LANES, LANES)], sems.at[n]).start()
    for n, out in enumerate((sol, res)):
        pltpu.make_async_copy(out, out, sems.at[n]).wait()


def kernel(
    src, coef, guess, places, parts,
    stage, s1b, s1g, s1r, g1b, g1g, g1r, dup, s2b, s2g, s2r, s2k, g2b, g2g, g2r, g2k,
    ext, red, faces, diag, inverse, black_res, ysend, yrecv, xrecv, crecv, place, found, inv,
    in_sem, s1_sem, r1_sem, s2_sem, r2_sem, hs_sem, hr_sem, place_sem, inv_sem,
):
    i = lax.axis_index("bx")
    j = lax.axis_index("by")
    me = i * NY + j
    s1, g1 = (s1b, s1g, s1r), (g1b, g1g, g1r)
    s2, g2 = (s2b, s2g, s2r, s2k), (g2b, g2g, g2r, g2k)
    lane = lax.broadcasted_iota(jnp.int32, (8, LANES), 1)
    low = lane < 64

    def device(t):
        return t >> 4, t & (NY - 1)

    loads = [
        pltpu.make_async_copy(ref, stage.at[f], in_sem.at[f])
        for f, ref in enumerate((coef, guess, src))
    ]
    for load in loads:
        load.start()
    place_load = pltpu.make_async_copy(places, place, place_sem)
    place_load.start()

    barrier = pltpu.get_barrier_semaphore()

    def greet(s, _):
        pl.semaphore_signal(barrier, inc=1, device_id=device((me + s) & (ND - 1)), device_id_type=MESH)
        return 0

    lax.fori_loop(1, ND, greet, 0, unroll=7)

    def packed(f, q):
        cols = pl.ds(pl.multiple_of(q * LANES, LANES), LANES)
        first, second = stage[f, 0:8, cols], stage[f, 8:16, cols]
        even = jnp.where(low, first, pltpu.roll(second, 64, 1))
        odd = jnp.where(low, pltpu.roll(first, 64, 1), second)
        mask = (lane + q // 32) % 2 == 0
        return jnp.where(mask, even, odd), jnp.where(mask, odd, even)

    def pack_beta(q, _):
        r, k = packed(0, q)
        s1b[q, 0:8, :] = k
        s1b[q, 8:16, :] = r
        return 0

    def pack_guess(q, _):
        s1g[q, :, :] = packed(1, q)[1]
        return 0

    def pack_rhs(q, _):
        r, k = packed(2, q)
        s1r[q, 0:8, :] = r
        s1r[q, 8:16, :] = k
        return 0

    for f, pack in enumerate((pack_beta, pack_guess, pack_rhs)):
        loads[f].wait()
        lax.fori_loop(0, ND, pack, 0, unroll=8)
        if f == 0:
            pl.semaphore_wait(barrier, ND - 1)

        def spread(s, _, f=f):
            t = (me + s * STRIDE) & (ND - 1)
            pltpu.make_async_remote_copy(
                s1[f].at[t], g1[f].at[me], s1_sem.at[f], r1_sem.at[f], device_id=device(t), device_id_type=MESH
            ).start()
            return 0

        pltpu.make_async_copy(s1[f].at[me], g1[f].at[me], r1_sem.at[f]).start()
        lax.fori_loop(1, ND, spread, 0, unroll=7)

    position = lax.broadcasted_iota(jnp.int32, (NX * 2, LANES), 0) * LANES
    position = position + lax.broadcasted_iota(jnp.int32, (NX * 2, LANES), 1)

    def find(b, boxes):
        return jnp.where(position == place[b], b, boxes)

    place_load.wait()
    found[...] = lax.fori_loop(0, ND * 16, find, jnp.zeros((NX * 2, LANES), jnp.int32), unroll=16)
    indices = pltpu.make_async_copy(found, inv, inv_sem)
    indices.start()
    indices.wait()

    low_row = lax.broadcasted_iota(jnp.int32, (1, LANES), 1) < 64
    for u, (_, count, f) in enumerate(UNITS):
        rows_sent = 8 * count
        doubled = u - f
        if not doubled:
            planes = g1[f].shape[1] // 8
            pltpu.make_async_copy(g1[f], g1[f], r1_sem.at[f]).wait()

            def double(d, _, f=f, planes=planes):
                for p in range(planes):
                    rows = g1[f][d, p * 8 : p * 8 + 8, :]
                    other = pltpu.roll(rows, 64, 1)
                    at = pl.multiple_of(d * 16, 16)
                    dup[p, pl.ds(at, 8), :] = jnp.where(low, rows, other)
                    dup[p, pl.ds(at + 8, 8), :] = jnp.where(low, other, rows)
                return 0

            lax.fori_loop(0, ND, double, 0, unroll=8)

        def gather(t, u=u, count=count, doubled=doubled):
            ti, tj = device(t)
            for tx in range(2):
                for m in range(4):
                    a = inv[ti * 2 + tx, tj * 8 + 2 * m]
                    b = inv[ti * 2 + tx, tj * 8 + 2 * m + 1]
                    for p in range(count):
                        row = jnp.where(low_row, dup[doubled + p, pl.ds(a, 1), :], dup[doubled + p, pl.ds(b, 1), :])
                        s2[u][t, pl.ds(p * 8 + tx * 4 + m, 1), :] = row

        def send(t, u=u, rows_sent=rows_sent):
            pltpu.make_async_remote_copy(
                s2[u].at[t], g2[u].at[pl.ds(me * rows_sent, rows_sent)], s2_sem.at[u], r2_sem.at[u],
                device_id=device(t), device_id_type=MESH,
            ).start()

        def group(first, number, gather=gather, send=send):
            tiles = [(me + (first + n) * STRIDE) & (ND - 1) for n in range(number)]
            for t in tiles:
                gather(t)
            for t in tiles:
                send(t)

        def send_group(n, _, group=group):
            group(1 + n * GROUP, GROUP)
            return 0

        lax.fori_loop(0, (ND - 1) // GROUP, send_group, 0)
        group(1 + (ND - 1) // GROUP * GROUP, (ND - 1) % GROUP)
        gather(me)
        pltpu.make_async_copy(s2[u].at[me], g2[u].at[pl.ds(me * rows_sent, rows_sent)], r2_sem.at[u]).start()

    up, down = lax.rem(i + NX - 1, NX), lax.rem(i + 1, NX)
    left, right = lax.rem(j + NY - 1, NY), lax.rem(j + 1, NY)

    def halo_copies(u):
        first, count, _ = UNITS[u]
        planes = pl.ds(first, count)
        copies = []

        def add(source, target, device):
            n = len(copies)
            copies.append(
                pltpu.make_async_remote_copy(
                    source, target, hs_sem.at[u, n], hr_sem.at[u, n], device_id=device, device_id_type=MESH
                )
            )

        for side, device in enumerate(((i, left), (i, right))):
            add(ysend.at[planes, side], yrecv.at[planes, side], device)
        for side, (start, row) in enumerate(((0, up), (56, down))):
            rows = pl.ds(start, 8)
            add(ext.at[planes, :, rows, pl.ds(0, 4 * LANES)], xrecv.at[planes, side], (row, j))
            for way, (at, col) in enumerate(((0, left), (3 * LANES, right))):
                add(ext.at[planes, :, rows, pl.ds(at, LANES)], crecv.at[planes, side, way], (row, col))
        return copies

    def lay_out(u):
        pltpu.make_async_copy(g2[u], g2[u], r2_sem.at[u]).wait()
        first, count, _ = UNITS[u]
        for p in range(count):
            for z in range(BZ):
                for tile in range(OWN_TILES):
                    start = (z * 32 + tile % 4 * 8) * 8 * count + p * 8 + tile // 4 * 4
                    for m in range(4):
                        ext[first + p, z, tile * 8 : tile * 8 + 8, m * LANES : (m + 1) * LANES] = g2[u][
                            pl.ds(start + m, 8, stride=8 * count), :
                        ]
            for g in range(2):
                to_left = jnp.zeros((8, LANES), F32)
                to_right = jnp.zeros((8, LANES), F32)
                for c in range(16):
                    z, tile = divmod(g * 16 + c, OWN_TILES)
                    rows = slice(tile * 8, tile * 8 + 8)
                    mask = lane // 8 == c
                    head = ext[first + p, z, rows, 0:LANES]
                    tail = ext[first + p, z, rows, 3 * LANES : 4 * LANES]
                    to_left = jnp.where(mask, pltpu.roll(head, 8 * c, 1), to_left)
                    to_right = jnp.where(mask, pltpu.roll(tail, (8 * c + 8) % LANES, 1), to_right)
                ysend[first + p, 0, g] = to_left
                ysend[first + p, 1, g] = to_right
        for copy in halo_copies(u):
            copy.start()

    from_right = (lane < 8) & (j < NY - 1)
    from_left = (lane >= 120) & (j > 0)
    row = lax.broadcasted_iota(jnp.int32, (8, COLS), 0)
    from_below = (row < 4) & (i < NX - 1)
    from_above = (row >= 4) & (i > 0)

    def merge(u):
        first, count, _ = UNITS[u]
        for copy in halo_copies(u):
            copy.wait_recv()
        for p in range(first, first + count):
            for n in range(BZ * OWN_TILES):
                g, c = divmod(n, 16)
                z, tile = divmod(n, OWN_TILES)
                head = pltpu.roll(yrecv[p, 0, g], (LANES - 8 * c) % LANES, 1)
                tail = pltpu.roll(yrecv[p, 1, g], 120 - 8 * c, 1)
                ext[p, z, tile * 8 : tile * 8 + 8, 4 * LANES :] = jnp.where(
                    from_right, head, jnp.where(from_left, tail, 0.0)
                )
            for z in range(BZ):
                edge = slice(0, LANES)
                for m in range(4):
                    part = slice(m * LANES, (m + 1) * LANES)
                    ext[p, z, 64:72, part] = jnp.where(
                        from_below[:, edge],
                        xrecv[p, 0, z, :, part],
                        jnp.where(from_above[:, edge], xrecv[p, 1, z, :, part], 0.0),
                    )
                corner = [
                    jnp.where(from_right, crecv[p, side, 0, z], jnp.where(from_left, crecv[p, side, 1, z], 0.0))
                    for side in range(2)
                ]
                ext[p, z, 64:72, 4 * LANES :] = jnp.where(
                    from_below[:, edge], corner[0], jnp.where(from_above[:, edge], corner[1], 0.0)
                )

    column = lax.broadcasted_iota(jnp.int32, (8, COLS), 1)

    def tile_rows(tile):
        return pl.ds(pl.multiple_of(tile * 8, 8), 8)

    def neighbours(ref, colour, z, tile):
        here = tile_rows(tile)
        current = ref[z, here, :]
        before = ref[z, tile_rows(lax.rem(tile + TILES - 1, TILES)), :]
        after = ref[z, tile_rows(lax.rem(tile + 1, TILES)), :]
        minus = jnp.where(row == 0, pltpu.roll(before, 1, 0), pltpu.roll(current, 1, 0))
        plus = jnp.where(row == 7, pltpu.roll(after, 7, 0), pltpu.roll(current, 7, 0))
        even_x = (column + z) % 2 == colour
        return (
            ref[z - 1, here, :] if z > 0 else None,
            ref[z + 1, here, :] if z < BZ - 1 else None,
            current,
            jnp.where(even_x, minus, plus),
            pltpu.roll(current, 1, 1),
            pltpu.roll(current, COLS - 1, 1),
        )

    def make_faces(tile, _):
        here = tile_rows(tile)
        for colour in range(2):
            centre_ref, other_ref = (ext.at[BETA_R], ext.at[BETA_K]) if colour == 0 else (ext.at[BETA_K], ext.at[BETA_R])
            for z in range(BZ):
                centre = centre_ref[z, here, :]
                total = None
                for n, value in enumerate(neighbours(other_ref, colour, z, tile)):
                    face = 0.5 * centre if value is None else 0.5 * (centre + value)
                    if value is not None:
                        faces[colour, n, z, here, :] = face
                    total = face if total is None else total + face
                inside = centre > 0.0
                diag[colour, z, here, :] = total
                inverse[colour, z, here, :] = jnp.where(inside, 1.0 / jnp.where(inside, total, 1.0), 0.0)
        return 0

    def pulled(colour, other_ref, rhs_plane, z, tile):
        here = tile_rows(tile)
        total = ext[rhs_plane, z, here, :]
        for n, value in enumerate(neighbours(other_ref, colour, z, tile)):
            if value is not None:
                total = total + faces[colour, n, z, here, :] * value
        return total

    def update_red(tile, _):
        here = tile_rows(tile)
        for z in range(BZ):
            red[z, here, :] = pulled(0, ext.at[PHI_K], RHS_R, z, tile) * inverse[0, z, here, :]
        return 0

    def update_black(tile, _):
        here = tile_rows(tile)
        for z in range(BZ):
            ext[PHI_K, z, here, :] = pulled(1, red, RHS_K, z, tile) * inverse[1, z, here, :]
        return 0

    own = 4 * LANES

    def write(out, z, tile, red_part, black_part):
        even_x = (column[:, :own] + z) % 2 == 0
        start = pl.multiple_of(tile * 16, 16)
        even, odd = jnp.where(even_x, red_part, black_part), jnp.where(even_x, black_part, red_part)
        for m in range(4):
            part = slice(m * LANES, (m + 1) * LANES)
            parts[out, z, m, pl.ds(start, 8, stride=2), :] = even[:, part]
            parts[out, z, m, pl.ds(start + 1, 8, stride=2), :] = odd[:, part]

    def last_black(tile, _):
        here = tile_rows(tile)
        for z in range(BZ):
            total = pulled(1, red, RHS_K, z, tile)
            value = total * inverse[1, z, here, :]
            ext[PHI_K, z, here, :] = value
            black_res[z, here, :] = total - diag[1, z, here, :] * value
        return 0

    def outputs(tile, _):
        here = tile_rows(tile)
        for z in range(BZ):
            red_value = red[z, here, :]
            total = pulled(0, ext.at[PHI_K], RHS_R, z, tile)
            red_res = total - diag[0, z, here, :] * red_value
            write(0, z, tile, red_value[:, :own], ext[PHI_K, z, here, :][:, :own])
            write(1, z, tile, red_res[:, :own], black_res[z, here, :][:, :own])
        return 0

    for u in range(4):
        lay_out(u)
    merge(0)
    lax.fori_loop(0, TILES, make_faces, 0)
    merge(1)
    merge(2)
    lax.fori_loop(0, TILES, update_red, 0)
    merge(3)
    for copy in halo_copies(1):
        copy.wait_send()
    for sweep in range(SWEEPS):
        if sweep > 0:
            lax.fori_loop(0, TILES, update_red, 0)
        lax.fori_loop(0, TILES, update_black if sweep < SWEEPS - 1 else last_black, 0)
    lax.fori_loop(0, OWN_TILES, outputs, 0)

    for f in range(3):
        part = s1[f].at[pl.ds(0, ND - 1)]
        pltpu.make_async_copy(part, part, s1_sem.at[f]).wait()
    for u in range(4):
        part = s2[u].at[pl.ds(0, ND - 1)]
        pltpu.make_async_copy(part, part, s2_sem.at[u]).wait()
        if u != 1:
            for copy in halo_copies(u):
                copy.wait_send()


def local(source, coefficient, initial_guess, box_place):
    vmem, dma = pltpu.VMEM, pltpu.SemaphoreType.DMA
    plane = (BZ, ROWS, COLS)
    any_spec = pl.BlockSpec(memory_space=pl.ANY)
    inputs = [pltpu.with_memory_space_constraint(x, pltpu.HBM) for x in (source, coefficient, initial_guess, box_place)]
    parts = pl.pallas_call(
        kernel,
        out_shape=jax.ShapeDtypeStruct((2, BZ, 4, 128, LANES), F32),
        in_specs=[any_spec] * 4,
        out_specs=pl.BlockSpec(memory_space=pltpu.VMEM),
        scratch_shapes=[
            vmem((3, 16, 16384), F32),
            *[vmem((ND, rows, LANES), F32) for rows in (16, 8, 16)],
            *[vmem((ND, rows, LANES), F32) for rows in (16, 8, 16)],
            vmem((2, ND * 16, LANES), F32),
            *[vmem((ND, rows, LANES), F32) for rows in (16, 8, 8, 8)],
            *[vmem((ND * rows, LANES), F32) for rows in (16, 8, 8, 8)],
            vmem((5, *plane), F32),
            vmem(plane, F32),
            vmem((2, 6, *plane), F32),
            vmem((2, *plane), F32),
            vmem((2, *plane), F32),
            vmem(plane, F32),
            vmem((5, 2, 2, 8, LANES), F32),
            vmem((5, 2, 2, 8, LANES), F32),
            vmem((5, 2, BZ, 8, 4 * LANES), F32),
            vmem((5, 2, 2, BZ, 8, LANES), F32),
            pltpu.SMEM((ND * 16,), jnp.int32),
            vmem((NX * 2, LANES), jnp.int32),
            pltpu.SMEM((NX * 2, LANES), jnp.int32),
            dma((3,)),
            dma((3,)),
            dma((3,)),
            dma((4,)),
            dma((4,)),
            dma((4, 8)),
            dma((4, 8)),
            dma,
            dma,
        ],
        compiler_params=pltpu.CompilerParams(
            collective_id=0, has_side_effects=True, vmem_limit_bytes=48 << 20
        ),
    )(*inputs)
    return pl.pallas_call(
        store_kernel,
        out_shape=(jax.ShapeDtypeStruct((BZ, 128, 512), F32),) * 2,
        in_specs=[any_spec],
        out_specs=(any_spec,) * 2,
        scratch_shapes=[dma((2,))],
        compiler_params=pltpu.CompilerParams(vmem_limit_bytes=4 << 20),
    )(parts)


def solution(mesh):
    boxes = P(("bx", "by"), None)
    out = P(None, "bx", "by")
    return jax.shard_map(
        local,
        mesh=mesh,
        in_specs=(boxes, boxes, boxes, P()),
        out_specs=(out, out),
        check_vma=False,
    )
```

```python
import jax
import jax.numpy as jnp
from jax import lax
from jax.experimental import pallas as pl
from jax.experimental.pallas import tpu as pltpu
from jax.sharding import PartitionSpec as P

MESH = pl.DeviceIdType.MESH
F32 = jnp.float32
NX = 8
NY = 16
ND = NX * NY
BZ = 4
LANES = 128
ROWS = 72
COLS = 640
OWN_TILES = 8
TILES = ROWS // 8
STRIDE = 45
GROUP = 8

BETA_K, BETA_R, PHI_K, RHS_R, RHS_K = range(5)
UNITS = ((0, 2, 0), (2, 1, 1), (3, 1, 2), (4, 1, 2))


def store_kernel(parts, sol, res, sems):
    for n, out in enumerate((sol, res)):
        for m in range(4):
            pltpu.make_async_copy(parts.at[n, :, m], out.at[:, :, pl.ds(m * LANES, LANES)], sems.at[n]).start()
    for n, out in enumerate((sol, res)):
        pltpu.make_async_copy(out, out, sems.at[n]).wait()


def kernel(
    src, coef, guess, places, parts,
    stage, s1b, s1g, s1r, g1b, g1g, g1r, dup, s2b, s2g, s2r, s2k, g2b, g2g, g2r, g2k,
    ext, red, faces, diag, inverse, black_res, ysend, xsend, yrecv, xrecv, crecv, place, found, inv,
    in_sem, s1_sem, r1_sem, s2_sem, r2_sem, hs_sem, hr_sem, place_sem, inv_sem,
):
    i = lax.axis_index("bx")
    j = lax.axis_index("by")
    me = i * NY + j
    s1, g1 = (s1b, s1g, s1r), (g1b, g1g, g1r)
    s2, g2 = (s2b, s2g, s2r, s2k), (g2b, g2g, g2r, g2k)
    lane = lax.broadcasted_iota(jnp.int32, (8, LANES), 1)
    low = lane < 64

    def device(t):
        return t >> 4, t & (NY - 1)

    barrier = pltpu.get_barrier_semaphore()

    def greet(s, _):
        pl.semaphore_signal(barrier, inc=1, device_id=device((me + s) & (ND - 1)), device_id_type=MESH)
        return 0

    lax.fori_loop(1, ND, greet, 0, unroll=7)

    loads = [
        pltpu.make_async_copy(ref, stage.at[f], in_sem.at[f])
        for f, ref in enumerate((coef, guess, src))
    ]
    for load in loads:
        load.start()
    place_load = pltpu.make_async_copy(places, place, place_sem)
    place_load.start()

    def packed(f, q):
        cols = pl.ds(pl.multiple_of(q * LANES, LANES), LANES)
        first, second = stage[f, 0:8, cols], stage[f, 8:16, cols]
        even = jnp.where(low, first, pltpu.roll(second, 64, 1))
        odd = jnp.where(low, pltpu.roll(first, 64, 1), second)
        mask = (lane + q // 32) % 2 == 0
        return jnp.where(mask, even, odd), jnp.where(mask, odd, even)

    def pack_beta(q):
        r, k = packed(0, q)
        s1b[q, 0:8, :] = k
        s1b[q, 8:16, :] = r

    def pack_guess(q):
        s1g[q, :, :] = packed(1, q)[1]

    def pack_rhs(q):
        r, k = packed(2, q)
        s1r[q, 0:8, :] = r
        s1r[q, 8:16, :] = k

    pl.semaphore_wait(barrier, ND - 1)
    for f, pack in enumerate((pack_beta, pack_guess, pack_rhs)):
        loads[f].wait()

        def spread(first, number, f=f, pack=pack):
            tiles = [(me + (first + n) * STRIDE) & (ND - 1) for n in range(number)]
            for t in tiles:
                pack(t)
            for t in tiles:
                pltpu.make_async_remote_copy(
                    s1[f].at[t], g1[f].at[me], s1_sem.at[f], r1_sem.at[f], device_id=device(t), device_id_type=MESH
                ).start()

        def spread_group(n, _, spread=spread):
            spread(1 + n * GROUP, GROUP)
            return 0

        lax.fori_loop(0, (ND - 1) // GROUP, spread_group, 0)
        spread(1 + (ND - 1) // GROUP * GROUP, (ND - 1) % GROUP)
        pack(me)
        pltpu.make_async_copy(s1[f].at[me], g1[f].at[me], r1_sem.at[f]).start()

    position = lax.broadcasted_iota(jnp.int32, (NX * 2, LANES), 0) * LANES
    position = position + lax.broadcasted_iota(jnp.int32, (NX * 2, LANES), 1)

    def find(b, boxes):
        return jnp.where(position == place[b], b, boxes)

    place_load.wait()
    found[...] = lax.fori_loop(0, ND * 16, find, jnp.zeros((NX * 2, LANES), jnp.int32), unroll=16)
    indices = pltpu.make_async_copy(found, inv, inv_sem)
    indices.start()
    indices.wait()

    low_row = lax.broadcasted_iota(jnp.int32, (1, LANES), 1) < 64
    for u, (_, count, f) in enumerate(UNITS):
        rows_sent = 8 * count
        doubled = u - f
        if not doubled:
            planes = g1[f].shape[1] // 8
            pltpu.make_async_copy(g1[f], g1[f], r1_sem.at[f]).wait()

            def double(d, _, f=f, planes=planes):
                for p in range(planes):
                    rows = g1[f][d, p * 8 : p * 8 + 8, :]
                    other = pltpu.roll(rows, 64, 1)
                    at = pl.multiple_of(d * 16, 16)
                    dup[p, pl.ds(at, 8), :] = jnp.where(low, rows, other)
                    dup[p, pl.ds(at + 8, 8), :] = jnp.where(low, other, rows)
                return 0

            lax.fori_loop(0, ND, double, 0, unroll=8)

        def gather(t, u=u, count=count, doubled=doubled):
            ti, tj = device(t)
            for tx in range(2):
                for m in range(4):
                    a = inv[ti * 2 + tx, tj * 8 + 2 * m]
                    b = inv[ti * 2 + tx, tj * 8 + 2 * m + 1]
                    for p in range(count):
                        row = jnp.where(low_row, dup[doubled + p, pl.ds(a, 1), :], dup[doubled + p, pl.ds(b, 1), :])
                        s2[u][t, pl.ds(p * 8 + tx * 4 + m, 1), :] = row

        def send(t, u=u, rows_sent=rows_sent):
            pltpu.make_async_remote_copy(
                s2[u].at[t], g2[u].at[pl.ds(me * rows_sent, rows_sent)], s2_sem.at[u], r2_sem.at[u],
                device_id=device(t), device_id_type=MESH,
            ).start()

        def group(first, number, gather=gather, send=send):
            tiles = [(me + (first + n) * STRIDE) & (ND - 1) for n in range(number)]
            for t in tiles:
                gather(t)
            for t in tiles:
                send(t)

        def send_group(n, _, group=group):
            group(1 + n * GROUP, GROUP)
            return 0

        lax.fori_loop(0, (ND - 1) // GROUP, send_group, 0)
        group(1 + (ND - 1) // GROUP * GROUP, (ND - 1) % GROUP)
        gather(me)
        pltpu.make_async_copy(s2[u].at[me], g2[u].at[pl.ds(me * rows_sent, rows_sent)], r2_sem.at[u]).start()

    up, down = lax.rem(i + NX - 1, NX), lax.rem(i + 1, NX)
    left, right = lax.rem(j + NY - 1, NY), lax.rem(j + 1, NY)

    def halo_copies(u):
        first, count, _ = UNITS[u]
        planes = pl.ds(first, count)
        copies = []

        def add(source, target, device):
            n = len(copies)
            copies.append(
                pltpu.make_async_remote_copy(
                    source, target, hs_sem.at[u, n], hr_sem.at[u, n], device_id=device, device_id_type=MESH
                )
            )

        for side, device in enumerate(((i, left), (i, right))):
            add(ysend.at[planes, side], yrecv.at[planes, side], device)
        for side, row in enumerate((up, down)):
            add(xsend.at[planes, side], xrecv.at[planes, side], (row, j))
            for way, col in enumerate((left, right)):
                add(ysend.at[planes, way], crecv.at[planes, side, way], (row, col))
        return copies

    upper = lax.broadcasted_iota(jnp.int32, (8, LANES), 0) < 4

    def lay_out(u):
        pltpu.make_async_copy(g2[u], g2[u], r2_sem.at[u]).wait()
        first, count, _ = UNITS[u]
        for p in range(count):
            for z in range(BZ):
                for tile in range(OWN_TILES):
                    start = (z * 32 + tile % 4 * 8) * 8 * count + p * 8 + tile // 4 * 4
                    for m in range(4):
                        ext[first + p, z, tile * 8 : tile * 8 + 8, m * LANES : (m + 1) * LANES] = g2[u][
                            pl.ds(start + m, 8, stride=8 * count), :
                        ]
            for g in range(2):
                to_left = jnp.zeros((8, LANES), F32)
                to_right = jnp.zeros((8, LANES), F32)
                for c in range(16):
                    z, tile = divmod(g * 16 + c, OWN_TILES)
                    rows = slice(tile * 8, tile * 8 + 8)
                    mask = lane // 8 == c
                    head = ext[first + p, z, rows, 0:LANES]
                    tail = ext[first + p, z, rows, 3 * LANES : 4 * LANES]
                    to_left = jnp.where(mask, pltpu.roll(head, 8 * c, 1), to_left)
                    to_right = jnp.where(mask, pltpu.roll(tail, (8 * c + 8) % LANES, 1), to_right)
                ysend[first + p, 0, g] = to_left
                ysend[first + p, 1, g] = to_right
                for m in range(4):
                    part = slice(m * LANES, (m + 1) * LANES)
                    tops = [ext[first + p, z, 0:8, part] for z in (2 * g, 2 * g + 1)]
                    ends = [ext[first + p, z, 56:64, part] for z in (2 * g, 2 * g + 1)]
                    xsend[first + p, 0, g, :, part] = jnp.where(upper, tops[0], pltpu.roll(tops[1], 4, 0))
                    xsend[first + p, 1, g, :, part] = jnp.where(upper, pltpu.roll(ends[0], 4, 0), ends[1])
        for copy in halo_copies(u):
            copy.start()

    from_right = (lane < 8) & (j < NY - 1)
    from_left = (lane >= 120) & (j > 0)
    from_below = upper & (i < NX - 1)
    from_above = ~upper & (i > 0)

    def beside(head, tail, c):
        head = pltpu.roll(head, (LANES - 8 * c) % LANES, 1)
        tail = pltpu.roll(tail, 120 - 8 * c, 1)
        return jnp.where(from_right, head, jnp.where(from_left, tail, 0.0))

    def merge(u):
        first, count, _ = UNITS[u]
        for copy in halo_copies(u):
            copy.wait_recv()
        for p in range(first, first + count):
            for n in range(BZ * OWN_TILES):
                g, c = divmod(n, 16)
                z, tile = divmod(n, OWN_TILES)
                ext[p, z, tile * 8 : tile * 8 + 8, 4 * LANES :] = beside(yrecv[p, 0, g], yrecv[p, 1, g], c)
            for z in range(BZ):
                g, odd = divmod(z, 2)
                for m in range(4):
                    part = slice(m * LANES, (m + 1) * LANES)
                    below, above = xrecv[p, 0, g, :, part], xrecv[p, 1, g, :, part]
                    if odd:
                        below = pltpu.roll(below, 4, 0)
                    else:
                        above = pltpu.roll(above, 4, 0)
                    ext[p, z, 64:72, part] = jnp.where(from_below, below, jnp.where(from_above, above, 0.0))
                below, above = (
                    beside(crecv[p, side, 0, g], crecv[p, side, 1, g], 8 * odd + 7 * side) for side in range(2)
                )
                ext[p, z, 64:72, 4 * LANES :] = jnp.where(from_below, below, jnp.where(from_above, above, 0.0))

    row = lax.broadcasted_iota(jnp.int32, (8, COLS), 0)
    column = lax.broadcasted_iota(jnp.int32, (8, COLS), 1)

    def tile_rows(tile):
        return pl.ds(pl.multiple_of(tile * 8, 8), 8)

    def neighbours(ref, colour, z, tile):
        here = tile_rows(tile)
        current = ref[z, here, :]
        before = ref[z, tile_rows(lax.rem(tile + TILES - 1, TILES)), :]
        after = ref[z, tile_rows(lax.rem(tile + 1, TILES)), :]
        minus = jnp.where(row == 0, pltpu.roll(before, 1, 0), pltpu.roll(current, 1, 0))
        plus = jnp.where(row == 7, pltpu.roll(after, 7, 0), pltpu.roll(current, 7, 0))
        even_x = (column + z) % 2 == colour
        return (
            ref[z - 1, here, :] if z > 0 else None,
            ref[z + 1, here, :] if z < BZ - 1 else None,
            current,
            jnp.where(even_x, minus, plus),
            pltpu.roll(current, 1, 1),
            pltpu.roll(current, COLS - 1, 1),
        )

    def make_faces(tile, _):
        here = tile_rows(tile)
        for colour in range(2):
            centre_ref, other_ref = (ext.at[BETA_R], ext.at[BETA_K]) if colour == 0 else (ext.at[BETA_K], ext.at[BETA_R])
            for z in range(BZ):
                centre = centre_ref[z, here, :]
                total = None
                for n, value in enumerate(neighbours(other_ref, colour, z, tile)):
                    face = 0.5 * centre if value is None else 0.5 * (centre + value)
                    if value is not None:
                        faces[colour, n, z, here, :] = face
                    total = face if total is None else total + face
                inside = centre > 0.0
                diag[colour, z, here, :] = total
                inverse[colour, z, here, :] = jnp.where(inside, 1.0 / jnp.where(inside, total, 1.0), 0.0)
        return 0

    def pulled(colour, other_ref, rhs_plane, z, tile):
        here = tile_rows(tile)
        total = ext[rhs_plane, z, here, :]
        for n, value in enumerate(neighbours(other_ref, colour, z, tile)):
            if value is not None:
                total = total + faces[colour, n, z, here, :] * value
        return total

    def update_red(tile, _):
        here = tile_rows(tile)
        for z in range(BZ):
            red[z, here, :] = pulled(0, ext.at[PHI_K], RHS_R, z, tile) * inverse[0, z, here, :]
        return 0

    own = 4 * LANES

    def black_own(tile, _):
        here = tile_rows(tile)
        for z in range(BZ):
            value = pulled(1, red, RHS_K, z, tile) * inverse[1, z, here, :]
            ext[PHI_K, z, here, :own] = value[:, :own]
        return 0

    def black_side(tile, _):
        here = tile_rows(tile)
        before, after = tile_rows(lax.rem(tile + TILES - 1, TILES)), tile_rows(lax.rem(tile + 1, TILES))
        side = slice(own, COLS)
        for z in range(BZ):
            current = red[z, here, side]
            minus = jnp.where(row[:, side] == 0, pltpu.roll(red[z, before, side], 1, 0), pltpu.roll(current, 1, 0))
            plus = jnp.where(row[:, side] == 7, pltpu.roll(red[z, after, side], 7, 0), pltpu.roll(current, 7, 0))
            even_x = (column[:, side] + z) % 2 == 1
            earlier, later = red[z, here, own - LANES : own], red[z, here, 0:LANES]
            values = (
                red[z - 1, here, side] if z > 0 else None,
                red[z + 1, here, side] if z < BZ - 1 else None,
                current,
                jnp.where(even_x, minus, plus),
                jnp.where(lane == 0, pltpu.roll(earlier, 1, 1), pltpu.roll(current, 1, 1)),
                jnp.where(lane == LANES - 1, pltpu.roll(later, LANES - 1, 1), pltpu.roll(current, LANES - 1, 1)),
            )
            total = ext[RHS_K, z, here, side]
            for n, value in enumerate(values):
                if value is not None:
                    total = total + faces[1, n, z, here, side] * value
            ext[PHI_K, z, here, side] = total * inverse[1, z, here, side]
        return 0

    def write(out, z, tile, red_part, black_part):
        even_x = (column[:, :own] + z) % 2 == 0
        start = pl.multiple_of(tile * 16, 16)
        even, odd = jnp.where(even_x, red_part, black_part), jnp.where(even_x, black_part, red_part)
        for m in range(4):
            part = slice(m * LANES, (m + 1) * LANES)
            parts[out, z, m, pl.ds(start, 8, stride=2), :] = even[:, part]
            parts[out, z, m, pl.ds(start + 1, 8, stride=2), :] = odd[:, part]

    def last_black(tile, _):
        here = tile_rows(tile)
        for z in range(BZ):
            total = pulled(1, red, RHS_K, z, tile)
            value = total * inverse[1, z, here, :]
            ext[PHI_K, z, here, :] = value
            black_res[z, here, :] = total - diag[1, z, here, :] * value
        return 0

    def outputs(tile, _):
        here = tile_rows(tile)
        for z in range(BZ):
            red_value = red[z, here, :]
            total = pulled(0, ext.at[PHI_K], RHS_R, z, tile)
            red_res = total - diag[0, z, here, :] * red_value
            write(0, z, tile, red_value[:, :own], ext[PHI_K, z, here, :][:, :own])
            write(1, z, tile, red_res[:, :own], black_res[z, here, :][:, :own])
        return 0

    for u in range(4):
        lay_out(u)
    merge(0)
    lax.fori_loop(0, TILES, make_faces, 0)
    merge(1)
    merge(2)
    lax.fori_loop(0, TILES, update_red, 0, unroll=3)
    lax.fori_loop(0, OWN_TILES, black_own, 0, unroll=2)
    merge(3)
    lax.fori_loop(0, OWN_TILES, black_side, 0, unroll=4)
    black_own(OWN_TILES, 0)
    black_side(OWN_TILES, 0)
    lax.fori_loop(0, TILES, update_red, 0, unroll=3)
    lax.fori_loop(0, TILES, last_black, 0, unroll=3)
    lax.fori_loop(0, OWN_TILES, outputs, 0, unroll=2)

    for f in range(3):
        part = s1[f].at[pl.ds(0, ND - 1)]
        pltpu.make_async_copy(part, part, s1_sem.at[f]).wait()
    for u in range(4):
        part = s2[u].at[pl.ds(0, ND - 1)]
        pltpu.make_async_copy(part, part, s2_sem.at[u]).wait()
        for copy in halo_copies(u):
            copy.wait_send()


def local(source, coefficient, initial_guess, box_place):
    vmem, dma = pltpu.VMEM, pltpu.SemaphoreType.DMA
    plane = (BZ, ROWS, COLS)
    any_spec = pl.BlockSpec(memory_space=pl.ANY)
    inputs = [pltpu.with_memory_space_constraint(x, pltpu.HBM) for x in (source, coefficient, initial_guess, box_place)]
    parts = pl.pallas_call(
        kernel,
        out_shape=jax.ShapeDtypeStruct((2, BZ, 4, 128, LANES), F32),
        in_specs=[any_spec] * 4,
        out_specs=pl.BlockSpec(memory_space=pltpu.VMEM),
        scratch_shapes=[
            vmem((3, 16, 16384), F32),
            *[vmem((ND, rows, LANES), F32) for rows in (16, 8, 16)],
            *[vmem((ND, rows, LANES), F32) for rows in (16, 8, 16)],
            vmem((2, ND * 16, LANES), F32),
            *[vmem((ND, rows, LANES), F32) for rows in (16, 8, 8, 8)],
            *[vmem((ND * rows, LANES), F32) for rows in (16, 8, 8, 8)],
            vmem((5, *plane), F32),
            vmem(plane, F32),
            vmem((2, 6, *plane), F32),
            vmem((2, *plane), F32),
            vmem((2, *plane), F32),
            vmem(plane, F32),
            vmem((5, 2, 2, 8, LANES), F32),
            vmem((5, 2, 2, 8, 4 * LANES), F32),
            vmem((5, 2, 2, 8, LANES), F32),
            vmem((5, 2, 2, 8, 4 * LANES), F32),
            vmem((5, 2, 2, 2, 8, LANES), F32),
            pltpu.SMEM((ND * 16,), jnp.int32),
            vmem((NX * 2, LANES), jnp.int32),
            pltpu.SMEM((NX * 2, LANES), jnp.int32),
            dma((3,)),
            dma((3,)),
            dma((3,)),
            dma((4,)),
            dma((4,)),
            dma((4, 8)),
            dma((4, 8)),
            dma,
            dma,
        ],
        compiler_params=pltpu.CompilerParams(
            collective_id=0, has_side_effects=True, vmem_limit_bytes=48 << 20
        ),
    )(*inputs)
    return pl.pallas_call(
        store_kernel,
        out_shape=(jax.ShapeDtypeStruct((BZ, 128, 512), F32),) * 2,
        in_specs=[any_spec],
        out_specs=(any_spec,) * 2,
        scratch_shapes=[dma((2,))],
        compiler_params=pltpu.CompilerParams(vmem_limit_bytes=4 << 20),
    )(parts)


def solution(mesh):
    boxes = P(("bx", "by"), None)
    out = P(None, "bx", "by")
    return jax.shard_map(
        local,
        mesh=mesh,
        in_specs=(boxes, boxes, boxes, P()),
        out_specs=(out, out),
        check_vma=False,
    )
```

```python
import jax
import jax.numpy as jnp
from jax import lax
from jax.experimental import pallas as pl
from jax.experimental.pallas import tpu as pltpu
from jax.sharding import PartitionSpec as P

MESH = pl.DeviceIdType.MESH
F32 = jnp.float32
NX = 8
NY = 16
ND = NX * NY
BZ = 4
LANES = 128
ROWS = 72
COLS = 640
OWN_TILES = 8
TILES = ROWS // 8
STRIDE = 45
GROUP = 8

BETA_K, BETA_R, PHI_K, RHS_R, RHS_K = range(5)
UNITS = ((0, 2, 0), (2, 1, 1), (3, 1, 2), (4, 1, 2))


def store_kernel(parts, sol, res, sems):
    for n, out in enumerate((sol, res)):
        for m in range(4):
            pltpu.make_async_copy(parts.at[n, :, m], out.at[:, :, pl.ds(m * LANES, LANES)], sems.at[n]).start()
    for n, out in enumerate((sol, res)):
        pltpu.make_async_copy(out, out, sems.at[n]).wait()


def kernel(
    src, coef, guess, places, parts,
    stage, s1b, s1g, s1r, g1b, g1g, g1r, dup, s2b, s2g, s2r, s2k, g2b, g2g, g2r, g2k,
    ext, red, faces, diag, inverse, black_res, ysend, xsend, yrecv, xrecv, crecv, place, found, inv,
    in_sem, s1_sem, r1_sem, s2_sem, r2_sem, hs_sem, hr_sem, place_sem, inv_sem,
):
    i = lax.axis_index("bx")
    j = lax.axis_index("by")
    me = i * NY + j
    s1, g1 = (s1b, s1g, s1r), (g1b, g1g, g1r)
    s2, g2 = (s2b, s2g, s2r, s2k), (g2b, g2g, g2r, g2k)
    lane = lax.broadcasted_iota(jnp.int32, (8, LANES), 1)
    low = lane < 64

    def device(t):
        return t >> 4, t & (NY - 1)

    barrier = pltpu.get_barrier_semaphore()

    def greet(s, _):
        pl.semaphore_signal(barrier, inc=1, device_id=device((me + s) & (ND - 1)), device_id_type=MESH)
        return 0

    lax.fori_loop(1, ND, greet, 0, unroll=7)

    loads = [
        pltpu.make_async_copy(ref, stage.at[f], in_sem.at[f])
        for f, ref in enumerate((coef, guess, src))
    ]
    for load in loads:
        load.start()
    place_load = pltpu.make_async_copy(places, place, place_sem)
    place_load.start()

    def packed(f, q):
        cols = pl.ds(pl.multiple_of(q * LANES, LANES), LANES)
        first, second = stage[f, 0:8, cols], stage[f, 8:16, cols]
        even = jnp.where(low, first, pltpu.roll(second, 64, 1))
        odd = jnp.where(low, pltpu.roll(first, 64, 1), second)
        mask = (lane + q // 32) % 2 == 0
        return jnp.where(mask, even, odd), jnp.where(mask, odd, even)

    def pack_beta(q):
        r, k = packed(0, q)
        s1b[q, 0:8, :] = k
        s1b[q, 8:16, :] = r

    def pack_guess(q):
        s1g[q, :, :] = packed(1, q)[1]

    def pack_rhs(q):
        r, k = packed(2, q)
        s1r[q, 0:8, :] = r
        s1r[q, 8:16, :] = k

    pl.semaphore_wait(barrier, ND - 1)
    for f, pack in enumerate((pack_beta, pack_guess, pack_rhs)):
        loads[f].wait()

        def spread(first, number, f=f, pack=pack):
            tiles = [(me + (first + n) * STRIDE) & (ND - 1) for n in range(number)]
            for t in tiles:
                pack(t)
            for t in tiles:
                pltpu.make_async_remote_copy(
                    s1[f].at[t], g1[f].at[me], s1_sem.at[f], r1_sem.at[f], device_id=device(t), device_id_type=MESH
                ).start()

        def spread_group(n, _, spread=spread):
            spread(1 + n * GROUP, GROUP)
            return 0

        lax.fori_loop(0, (ND - 1) // GROUP, spread_group, 0)
        spread(1 + (ND - 1) // GROUP * GROUP, (ND - 1) % GROUP)
        pack(me)
        pltpu.make_async_copy(s1[f].at[me], g1[f].at[me], r1_sem.at[f]).start()

    position = lax.broadcasted_iota(jnp.int32, (NX * 2, LANES), 0) * LANES
    position = position + lax.broadcasted_iota(jnp.int32, (NX * 2, LANES), 1)

    def find(b, boxes):
        return jnp.where(position == place[b], b, boxes)

    place_load.wait()
    found[...] = lax.fori_loop(0, ND * 16, find, jnp.zeros((NX * 2, LANES), jnp.int32), unroll=16)
    indices = pltpu.make_async_copy(found, inv, inv_sem)
    indices.start()
    indices.wait()

    low_row = lax.broadcasted_iota(jnp.int32, (1, LANES), 1) < 64
    for u, (_, count, f) in enumerate(UNITS):
        rows_sent = 8 * count
        doubled = u - f
        if not doubled:
            planes = g1[f].shape[1] // 8
            pltpu.make_async_copy(g1[f], g1[f], r1_sem.at[f]).wait()

            def double(d, _, f=f, planes=planes):
                for p in range(planes):
                    rows = g1[f][d, p * 8 : p * 8 + 8, :]
                    other = pltpu.roll(rows, 64, 1)
                    at = pl.multiple_of(d * 16, 16)
                    dup[p, pl.ds(at, 8), :] = jnp.where(low, rows, other)
                    dup[p, pl.ds(at + 8, 8), :] = jnp.where(low, other, rows)
                return 0

            lax.fori_loop(0, ND, double, 0, unroll=8)

        def gather(t, u=u, count=count, doubled=doubled):
            ti, tj = device(t)
            for tx in range(2):
                for m in range(4):
                    a = inv[ti * 2 + tx, tj * 8 + 2 * m]
                    b = inv[ti * 2 + tx, tj * 8 + 2 * m + 1]
                    for p in range(count):
                        row = jnp.where(low_row, dup[doubled + p, pl.ds(a, 1), :], dup[doubled + p, pl.ds(b, 1), :])
                        s2[u][t, pl.ds(p * 8 + tx * 4 + m, 1), :] = row

        def send(t, u=u, rows_sent=rows_sent):
            pltpu.make_async_remote_copy(
                s2[u].at[t], g2[u].at[pl.ds(me * rows_sent, rows_sent)], s2_sem.at[u], r2_sem.at[u],
                device_id=device(t), device_id_type=MESH,
            ).start()

        def group(first, number, gather=gather, send=send):
            tiles = [(me + (first + n) * STRIDE) & (ND - 1) for n in range(number)]
            for t in tiles:
                gather(t)
            for t in tiles:
                send(t)

        def send_group(n, _, group=group):
            group(1 + n * GROUP, GROUP)
            return 0

        lax.fori_loop(0, (ND - 1) // GROUP, send_group, 0)
        group(1 + (ND - 1) // GROUP * GROUP, (ND - 1) % GROUP)
        gather(me)
        pltpu.make_async_copy(s2[u].at[me], g2[u].at[pl.ds(me * rows_sent, rows_sent)], r2_sem.at[u]).start()

    up, down = lax.rem(i + NX - 1, NX), lax.rem(i + 1, NX)
    left, right = lax.rem(j + NY - 1, NY), lax.rem(j + 1, NY)

    def halo_copies(u):
        first, count, _ = UNITS[u]
        planes = pl.ds(first, count)
        copies = []

        def add(source, target, device):
            n = len(copies)
            copies.append(
                pltpu.make_async_remote_copy(
                    source, target, hs_sem.at[u, n], hr_sem.at[u, n], device_id=device, device_id_type=MESH
                )
            )

        for side, device in enumerate(((i, left), (i, right))):
            add(ysend.at[planes, side], yrecv.at[planes, side], device)
        for side, row in enumerate((up, down)):
            add(xsend.at[planes, side], xrecv.at[planes, side], (row, j))
            for way, col in enumerate((left, right)):
                add(ysend.at[planes, way], crecv.at[planes, side, way], (row, col))
        return copies

    upper = lax.broadcasted_iota(jnp.int32, (8, LANES), 0) < 4

    def lay_out(u):
        pltpu.make_async_copy(g2[u], g2[u], r2_sem.at[u]).wait()
        first, count, _ = UNITS[u]
        for p in range(count):
            for z in range(BZ):
                for tile in range(OWN_TILES):
                    start = (z * 32 + tile % 4 * 8) * 8 * count + p * 8 + tile // 4 * 4
                    for m in range(4):
                        ext[first + p, z, tile * 8 : tile * 8 + 8, m * LANES : (m + 1) * LANES] = g2[u][
                            pl.ds(start + m, 8, stride=8 * count), :
                        ]
            for g in range(2):
                to_left = jnp.zeros((8, LANES), F32)
                to_right = jnp.zeros((8, LANES), F32)
                for c in range(16):
                    z, tile = divmod(g * 16 + c, OWN_TILES)
                    rows = slice(tile * 8, tile * 8 + 8)
                    mask = lane // 8 == c
                    head = ext[first + p, z, rows, 0:LANES]
                    tail = ext[first + p, z, rows, 3 * LANES : 4 * LANES]
                    to_left = jnp.where(mask, pltpu.roll(head, 8 * c, 1), to_left)
                    to_right = jnp.where(mask, pltpu.roll(tail, (8 * c + 8) % LANES, 1), to_right)
                ysend[first + p, 0, g] = to_left
                ysend[first + p, 1, g] = to_right
                for m in range(4):
                    part = slice(m * LANES, (m + 1) * LANES)
                    tops = [ext[first + p, z, 0:8, part] for z in (2 * g, 2 * g + 1)]
                    ends = [ext[first + p, z, 56:64, part] for z in (2 * g, 2 * g + 1)]
                    xsend[first + p, 0, g, :, part] = jnp.where(upper, tops[0], pltpu.roll(tops[1], 4, 0))
                    xsend[first + p, 1, g, :, part] = jnp.where(upper, pltpu.roll(ends[0], 4, 0), ends[1])
        for copy in halo_copies(u):
            copy.start()

    from_right = (lane < 8) & (j < NY - 1)
    from_left = (lane >= 120) & (j > 0)
    from_below = upper & (i < NX - 1)
    from_above = ~upper & (i > 0)

    def beside(head, tail, c):
        head = pltpu.roll(head, (LANES - 8 * c) % LANES, 1)
        tail = pltpu.roll(tail, 120 - 8 * c, 1)
        return jnp.where(from_right, head, jnp.where(from_left, tail, 0.0))

    def merge(u):
        first, count, _ = UNITS[u]
        for copy in halo_copies(u):
            copy.wait_recv()
        for p in range(first, first + count):
            for n in range(BZ * OWN_TILES):
                g, c = divmod(n, 16)
                z, tile = divmod(n, OWN_TILES)
                ext[p, z, tile * 8 : tile * 8 + 8, 4 * LANES :] = beside(yrecv[p, 0, g], yrecv[p, 1, g], c)
            for z in range(BZ):
                g, odd = divmod(z, 2)
                for m in range(4):
                    part = slice(m * LANES, (m + 1) * LANES)
                    below, above = xrecv[p, 0, g, :, part], xrecv[p, 1, g, :, part]
                    if odd:
                        below = pltpu.roll(below, 4, 0)
                    else:
                        above = pltpu.roll(above, 4, 0)
                    ext[p, z, 64:72, part] = jnp.where(from_below, below, jnp.where(from_above, above, 0.0))
                below, above = (
                    beside(crecv[p, side, 0, g], crecv[p, side, 1, g], 8 * odd + 7 * side) for side in range(2)
                )
                ext[p, z, 64:72, 4 * LANES :] = jnp.where(from_below, below, jnp.where(from_above, above, 0.0))

    row = lax.broadcasted_iota(jnp.int32, (8, COLS), 0)
    column = lax.broadcasted_iota(jnp.int32, (8, COLS), 1)

    def tile_rows(tile):
        return pl.ds(pl.multiple_of(tile * 8, 8), 8)

    def neighbours(ref, colour, z, tile):
        here = tile_rows(tile)
        current = ref[z, here, :]
        before = ref[z, tile_rows(lax.rem(tile + TILES - 1, TILES)), :]
        after = ref[z, tile_rows(lax.rem(tile + 1, TILES)), :]
        minus = jnp.where(row == 0, pltpu.roll(before, 1, 0), pltpu.roll(current, 1, 0))
        plus = jnp.where(row == 7, pltpu.roll(after, 7, 0), pltpu.roll(current, 7, 0))
        even_x = (column + z) % 2 == colour
        return (
            ref[z - 1, here, :] if z > 0 else None,
            ref[z + 1, here, :] if z < BZ - 1 else None,
            current,
            jnp.where(even_x, minus, plus),
            pltpu.roll(current, 1, 1),
            pltpu.roll(current, COLS - 1, 1),
        )

    def make_faces(tile, _):
        here = tile_rows(tile)
        for colour in range(2):
            centre_ref, other_ref = (ext.at[BETA_R], ext.at[BETA_K]) if colour == 0 else (ext.at[BETA_K], ext.at[BETA_R])
            for z in range(BZ):
                centre = centre_ref[z, here, :]
                total = None
                for n, value in enumerate(neighbours(other_ref, colour, z, tile)):
                    face = 0.5 * centre if value is None else 0.5 * (centre + value)
                    if value is not None:
                        faces[colour, n, z, here, :] = face
                    total = face if total is None else total + face
                inside = centre > 0.0
                diag[colour, z, here, :] = total
                inverse[colour, z, here, :] = jnp.where(inside, 1.0 / jnp.where(inside, total, 1.0), 0.0)
        return 0

    def pulled(colour, other_ref, rhs_plane, z, tile):
        here = tile_rows(tile)
        total = ext[rhs_plane, z, here, :]
        for n, value in enumerate(neighbours(other_ref, colour, z, tile)):
            if value is not None:
                total = total + faces[colour, n, z, here, :] * value
        return total

    def update_red(tile, _):
        here = tile_rows(tile)
        for z in range(BZ):
            red[z, here, :] = pulled(0, ext.at[PHI_K], RHS_R, z, tile) * inverse[0, z, here, :]
        return 0

    own = 4 * LANES

    def black_own(tile, _):
        here = tile_rows(tile)
        for z in range(BZ):
            value = pulled(1, red, RHS_K, z, tile) * inverse[1, z, here, :]
            ext[PHI_K, z, here, :own] = value[:, :own]
        return 0

    def black_side(tile, _):
        here = tile_rows(tile)
        before, after = tile_rows(lax.rem(tile + TILES - 1, TILES)), tile_rows(lax.rem(tile + 1, TILES))
        side = slice(own, COLS)
        for z in range(BZ):
            current = red[z, here, side]
            minus = jnp.where(row[:, side] == 0, pltpu.roll(red[z, before, side], 1, 0), pltpu.roll(current, 1, 0))
            plus = jnp.where(row[:, side] == 7, pltpu.roll(red[z, after, side], 7, 0), pltpu.roll(current, 7, 0))
            even_x = (column[:, side] + z) % 2 == 1
            earlier, later = red[z, here, own - LANES : own], red[z, here, 0:LANES]
            values = (
                red[z - 1, here, side] if z > 0 else None,
                red[z + 1, here, side] if z < BZ - 1 else None,
                current,
                jnp.where(even_x, minus, plus),
                jnp.where(lane == 0, pltpu.roll(earlier, 1, 1), pltpu.roll(current, 1, 1)),
                jnp.where(lane == LANES - 1, pltpu.roll(later, LANES - 1, 1), pltpu.roll(current, LANES - 1, 1)),
            )
            total = ext[RHS_K, z, here, side]
            for n, value in enumerate(values):
                if value is not None:
                    total = total + faces[1, n, z, here, side] * value
            ext[PHI_K, z, here, side] = total * inverse[1, z, here, side]
        return 0

    def write(out, z, tile, red_part, black_part):
        even_x = (column[:, :own] + z) % 2 == 0
        start = pl.multiple_of(tile * 16, 16)
        even, odd = jnp.where(even_x, red_part, black_part), jnp.where(even_x, black_part, red_part)
        for m in range(4):
            part = slice(m * LANES, (m + 1) * LANES)
            parts[out, z, m, pl.ds(start, 8, stride=2), :] = even[:, part]
            parts[out, z, m, pl.ds(start + 1, 8, stride=2), :] = odd[:, part]

    def last_black(tile, _):
        here = tile_rows(tile)
        for z in range(BZ):
            total = pulled(1, red, RHS_K, z, tile)
            value = total * inverse[1, z, here, :]
            ext[PHI_K, z, here, :] = value
            black_res[z, here, :] = total - diag[1, z, here, :] * value
        return 0

    def outputs(tile, _):
        here = tile_rows(tile)
        for z in range(BZ):
            red_value = red[z, here, :]
            total = pulled(0, ext.at[PHI_K], RHS_R, z, tile)
            red_res = total - diag[0, z, here, :] * red_value
            write(0, z, tile, red_value[:, :own], ext[PHI_K, z, here, :][:, :own])
            write(1, z, tile, red_res[:, :own], black_res[z, here, :][:, :own])
        return 0

    for u in range(4):
        lay_out(u)
    merge(0)
    lax.fori_loop(0, TILES, make_faces, 0)
    merge(1)
    merge(2)
    lax.fori_loop(0, TILES, update_red, 0, unroll=3)
    lax.fori_loop(0, OWN_TILES, black_own, 0, unroll=2)
    merge(3)
    lax.fori_loop(0, OWN_TILES, black_side, 0, unroll=4)
    black_own(OWN_TILES, 0)
    black_side(OWN_TILES, 0)
    lax.fori_loop(0, TILES, update_red, 0, unroll=9)
    lax.fori_loop(0, TILES, last_black, 0, unroll=9)
    lax.fori_loop(0, OWN_TILES, outputs, 0, unroll=4)

    for f in range(3):
        part = s1[f].at[pl.ds(0, ND - 1)]
        pltpu.make_async_copy(part, part, s1_sem.at[f]).wait()
    for u in range(4):
        part = s2[u].at[pl.ds(0, ND - 1)]
        pltpu.make_async_copy(part, part, s2_sem.at[u]).wait()
        for copy in halo_copies(u):
            copy.wait_send()


def local(source, coefficient, initial_guess, box_place):
    vmem, dma = pltpu.VMEM, pltpu.SemaphoreType.DMA
    plane = (BZ, ROWS, COLS)
    any_spec = pl.BlockSpec(memory_space=pl.ANY)
    inputs = [pltpu.with_memory_space_constraint(x, pltpu.HBM) for x in (source, coefficient, initial_guess, box_place)]
    parts = pl.pallas_call(
        kernel,
        out_shape=jax.ShapeDtypeStruct((2, BZ, 4, 128, LANES), F32),
        in_specs=[any_spec] * 4,
        out_specs=pl.BlockSpec(memory_space=pltpu.VMEM),
        scratch_shapes=[
            vmem((3, 16, 16384), F32),
            *[vmem((ND, rows, LANES), F32) for rows in (16, 8, 16)],
            *[vmem((ND, rows, LANES), F32) for rows in (16, 8, 16)],
            vmem((2, ND * 16, LANES), F32),
            *[vmem((ND, rows, LANES), F32) for rows in (16, 8, 8, 8)],
            *[vmem((ND * rows, LANES), F32) for rows in (16, 8, 8, 8)],
            vmem((5, *plane), F32),
            vmem(plane, F32),
            vmem((2, 6, *plane), F32),
            vmem((2, *plane), F32),
            vmem((2, *plane), F32),
            vmem(plane, F32),
            vmem((5, 2, 2, 8, LANES), F32),
            vmem((5, 2, 2, 8, 4 * LANES), F32),
            vmem((5, 2, 2, 8, LANES), F32),
            vmem((5, 2, 2, 8, 4 * LANES), F32),
            vmem((5, 2, 2, 2, 8, LANES), F32),
            pltpu.SMEM((ND * 16,), jnp.int32),
            vmem((NX * 2, LANES), jnp.int32),
            pltpu.SMEM((NX * 2, LANES), jnp.int32),
            dma((3,)),
            dma((3,)),
            dma((3,)),
            dma((4,)),
            dma((4,)),
            dma((4, 8)),
            dma((4, 8)),
            dma,
            dma,
        ],
        compiler_params=pltpu.CompilerParams(
            collective_id=0, has_side_effects=True, vmem_limit_bytes=48 << 20
        ),
    )(*inputs)
    return pl.pallas_call(
        store_kernel,
        out_shape=(jax.ShapeDtypeStruct((BZ, 128, 512), F32),) * 2,
        in_specs=[any_spec],
        out_specs=(any_spec,) * 2,
        scratch_shapes=[dma((2,))],
        compiler_params=pltpu.CompilerParams(vmem_limit_bytes=4 << 20),
    )(parts)


def solution(mesh):
    boxes = P(("bx", "by"), None)
    out = P(None, "bx", "by")
    return jax.shard_map(
        local,
        mesh=mesh,
        in_specs=(boxes, boxes, boxes, P()),
        out_specs=(out, out),
        check_vma=False,
    )
```

```python
import jax
import jax.numpy as jnp
from jax import lax
from jax.experimental import pallas as pl
from jax.experimental.pallas import tpu as pltpu
from jax.sharding import PartitionSpec as P

MESH = pl.DeviceIdType.MESH
F32 = jnp.float32
NX = 8
NY = 16
ND = NX * NY
BZ = 4
LANES = 128
ROWS = 72
COLS = 640
OWN_TILES = 8
TILES = ROWS // 8
STRIDE = 45
GROUP = 8

BETA_K, BETA_R, PHI_K, RHS_R, RHS_K = range(5)
UNITS = ((0, 2, 0), (2, 1, 1), (3, 1, 2), (4, 1, 2))


def store_kernel(parts, sol, res, sems):
    for n, out in enumerate((sol, res)):
        for m in range(4):
            pltpu.make_async_copy(parts.at[n, :, m], out.at[:, :, pl.ds(m * LANES, LANES)], sems.at[n]).start()
    for n, out in enumerate((sol, res)):
        pltpu.make_async_copy(out, out, sems.at[n]).wait()


def kernel(
    src, coef, guess, places, parts,
    stage, s1b, s1g, s1r, g1b, g1g, g1r, dup, s2b, s2g, s2r, s2k, g2b, g2g, g2r, g2k,
    ext, red, faces, diag, inverse, black_res, ysend, xsend, yrecv, xrecv, crecv, place, found, inv,
    in_sem, s1_sem, r1_sem, s2_sem, r2_sem, hs_sem, hr_sem, place_sem, inv_sem,
):
    i = lax.axis_index("bx")
    j = lax.axis_index("by")
    me = i * NY + j
    s1, g1 = (s1b, s1g, s1r), (g1b, g1g, g1r)
    s2, g2 = (s2b, s2g, s2r, s2k), (g2b, g2g, g2r, g2k)
    lane = lax.broadcasted_iota(jnp.int32, (8, LANES), 1)
    low = lane < 64

    def device(t):
        return t >> 4, t & (NY - 1)

    barrier = pltpu.get_barrier_semaphore()

    def greet(s, _):
        pl.semaphore_signal(barrier, inc=1, device_id=device((me + s) & (ND - 1)), device_id_type=MESH)
        return 0

    lax.fori_loop(1, ND, greet, 0, unroll=7)

    loads = [
        pltpu.make_async_copy(ref, stage.at[f], in_sem.at[f])
        for f, ref in enumerate((coef, guess, src))
    ]
    for load in loads:
        load.start()
    place_load = pltpu.make_async_copy(places, place, place_sem)
    place_load.start()

    def packed(f, q):
        cols = pl.ds(pl.multiple_of(q * LANES, LANES), LANES)
        first, second = stage[f, 0:8, cols], stage[f, 8:16, cols]
        even = jnp.where(low, first, pltpu.roll(second, 64, 1))
        odd = jnp.where(low, pltpu.roll(first, 64, 1), second)
        mask = (lane + q // 32) % 2 == 0
        return jnp.where(mask, even, odd), jnp.where(mask, odd, even)

    def pack_beta(q):
        r, k = packed(0, q)
        s1b[q, 0:8, :] = k
        s1b[q, 8:16, :] = r

    def pack_guess(q):
        s1g[q, :, :] = packed(1, q)[1]

    def pack_rhs(q):
        r, k = packed(2, q)
        s1r[q, 0:8, :] = r
        s1r[q, 8:16, :] = k

    pl.semaphore_wait(barrier, ND - 1)
    for f, pack in enumerate((pack_beta, pack_guess, pack_rhs)):
        loads[f].wait()

        def spread(first, number, f=f, pack=pack):
            tiles = [(me + (first + n) * STRIDE) & (ND - 1) for n in range(number)]
            for t in tiles:
                pack(t)
            for t in tiles:
                pltpu.make_async_remote_copy(
                    s1[f].at[t], g1[f].at[me], s1_sem.at[f], r1_sem.at[f], device_id=device(t), device_id_type=MESH
                ).start()

        def spread_group(n, _, spread=spread):
            spread(1 + n * GROUP, GROUP)
            return 0

        lax.fori_loop(0, (ND - 1) // GROUP, spread_group, 0)
        spread(1 + (ND - 1) // GROUP * GROUP, (ND - 1) % GROUP)
        pack(me)
        pltpu.make_async_copy(s1[f].at[me], g1[f].at[me], r1_sem.at[f]).start()

    position = lax.broadcasted_iota(jnp.int32, (NX * 2, LANES), 0) * LANES
    position = position + lax.broadcasted_iota(jnp.int32, (NX * 2, LANES), 1)

    def find(b, boxes):
        return jnp.where(position == place[b], b, boxes)

    place_load.wait()
    found[...] = lax.fori_loop(0, ND * 16, find, jnp.zeros((NX * 2, LANES), jnp.int32), unroll=16)
    indices = pltpu.make_async_copy(found, inv, inv_sem)
    indices.start()
    indices.wait()

    low_row = lax.broadcasted_iota(jnp.int32, (1, LANES), 1) < 64
    for u, (_, count, f) in enumerate(UNITS):
        rows_sent = 8 * count
        doubled = u - f
        if not doubled:
            planes = g1[f].shape[1] // 8
            pltpu.make_async_copy(g1[f], g1[f], r1_sem.at[f]).wait()

            def double(d, _, f=f, planes=planes):
                for p in range(planes):
                    rows = g1[f][d, p * 8 : p * 8 + 8, :]
                    other = pltpu.roll(rows, 64, 1)
                    at = pl.multiple_of(d * 16, 16)
                    dup[p, pl.ds(at, 8), :] = jnp.where(low, rows, other)
                    dup[p, pl.ds(at + 8, 8), :] = jnp.where(low, other, rows)
                return 0

            lax.fori_loop(0, ND, double, 0, unroll=8)

        def gather(t, u=u, count=count, doubled=doubled):
            ti, tj = device(t)
            for tx in range(2):
                for m in range(4):
                    a = inv[ti * 2 + tx, tj * 8 + 2 * m]
                    b = inv[ti * 2 + tx, tj * 8 + 2 * m + 1]
                    for p in range(count):
                        row = jnp.where(low_row, dup[doubled + p, pl.ds(a, 1), :], dup[doubled + p, pl.ds(b, 1), :])
                        s2[u][t, pl.ds(p * 8 + tx * 4 + m, 1), :] = row

        def send(t, u=u, rows_sent=rows_sent):
            pltpu.make_async_remote_copy(
                s2[u].at[t], g2[u].at[pl.ds(me * rows_sent, rows_sent)], s2_sem.at[u], r2_sem.at[u],
                device_id=device(t), device_id_type=MESH,
            ).start()

        def group(first, number, gather=gather, send=send):
            tiles = [(me + (first + n) * STRIDE) & (ND - 1) for n in range(number)]
            for t in tiles:
                gather(t)
            for t in tiles:
                send(t)

        def send_group(n, _, group=group):
            group(1 + n * GROUP, GROUP)
            return 0

        lax.fori_loop(0, (ND - 1) // GROUP, send_group, 0)
        group(1 + (ND - 1) // GROUP * GROUP, (ND - 1) % GROUP)
        gather(me)
        pltpu.make_async_copy(s2[u].at[me], g2[u].at[pl.ds(me * rows_sent, rows_sent)], r2_sem.at[u]).start()

    up, down = lax.rem(i + NX - 1, NX), lax.rem(i + 1, NX)
    left, right = lax.rem(j + NY - 1, NY), lax.rem(j + 1, NY)

    def halo_copies(u):
        first, count, _ = UNITS[u]
        planes = pl.ds(first, count)
        copies = []

        def add(source, target, device):
            n = len(copies)
            copies.append(
                pltpu.make_async_remote_copy(
                    source, target, hs_sem.at[u, n], hr_sem.at[u, n], device_id=device, device_id_type=MESH
                )
            )

        for side, row in enumerate((up, down)):
            add(xsend.at[planes, side], xrecv.at[planes, side], (row, j))
        for side, device in enumerate(((i, left), (i, right))):
            add(ysend.at[planes, side], yrecv.at[planes, side], device)
        for side, row in enumerate((up, down)):
            for way, col in enumerate((left, right)):
                add(ysend.at[planes, way], crecv.at[planes, side, way], (row, col))
        return copies

    upper = lax.broadcasted_iota(jnp.int32, (8, LANES), 0) < 4

    def lay_out(u):
        pltpu.make_async_copy(g2[u], g2[u], r2_sem.at[u]).wait()
        first, count, _ = UNITS[u]
        for p in range(count):
            for z in range(BZ):
                for tile in range(OWN_TILES):
                    start = (z * 32 + tile % 4 * 8) * 8 * count + p * 8 + tile // 4 * 4
                    for m in range(4):
                        ext[first + p, z, tile * 8 : tile * 8 + 8, m * LANES : (m + 1) * LANES] = g2[u][
                            pl.ds(start + m, 8, stride=8 * count), :
                        ]
            for g in range(2):
                to_left = jnp.zeros((8, LANES), F32)
                to_right = jnp.zeros((8, LANES), F32)
                for c in range(16):
                    z, tile = divmod(g * 16 + c, OWN_TILES)
                    rows = slice(tile * 8, tile * 8 + 8)
                    mask = lane // 8 == c
                    head = ext[first + p, z, rows, 0:LANES]
                    tail = ext[first + p, z, rows, 3 * LANES : 4 * LANES]
                    to_left = jnp.where(mask, pltpu.roll(head, 8 * c, 1), to_left)
                    to_right = jnp.where(mask, pltpu.roll(tail, (8 * c + 8) % LANES, 1), to_right)
                ysend[first + p, 0, g] = to_left
                ysend[first + p, 1, g] = to_right
                for m in range(4):
                    part = slice(m * LANES, (m + 1) * LANES)
                    tops = [ext[first + p, z, 0:8, part] for z in (2 * g, 2 * g + 1)]
                    ends = [ext[first + p, z, 56:64, part] for z in (2 * g, 2 * g + 1)]
                    xsend[first + p, 0, g, :, part] = jnp.where(upper, tops[0], pltpu.roll(tops[1], 4, 0))
                    xsend[first + p, 1, g, :, part] = jnp.where(upper, pltpu.roll(ends[0], 4, 0), ends[1])
        for copy in halo_copies(u):
            copy.start()

    from_right = (lane < 8) & (j < NY - 1)
    from_left = (lane >= 120) & (j > 0)
    from_below = upper & (i < NX - 1)
    from_above = ~upper & (i > 0)

    def beside(head, tail, c):
        head = pltpu.roll(head, (LANES - 8 * c) % LANES, 1)
        tail = pltpu.roll(tail, 120 - 8 * c, 1)
        return jnp.where(from_right, head, jnp.where(from_left, tail, 0.0))

    def merge(u):
        first, count, _ = UNITS[u]
        for copy in halo_copies(u):
            copy.wait_recv()
        for p in range(first, first + count):
            for n in range(BZ * OWN_TILES):
                g, c = divmod(n, 16)
                z, tile = divmod(n, OWN_TILES)
                ext[p, z, tile * 8 : tile * 8 + 8, 4 * LANES :] = beside(yrecv[p, 0, g], yrecv[p, 1, g], c)
            for z in range(BZ):
                g, odd = divmod(z, 2)
                for m in range(4):
                    part = slice(m * LANES, (m + 1) * LANES)
                    below, above = xrecv[p, 0, g, :, part], xrecv[p, 1, g, :, part]
                    if odd:
                        below = pltpu.roll(below, 4, 0)
                    else:
                        above = pltpu.roll(above, 4, 0)
                    ext[p, z, 64:72, part] = jnp.where(from_below, below, jnp.where(from_above, above, 0.0))
                below, above = (
                    beside(crecv[p, side, 0, g], crecv[p, side, 1, g], 8 * odd + 7 * side) for side in range(2)
                )
                ext[p, z, 64:72, 4 * LANES :] = jnp.where(from_below, below, jnp.where(from_above, above, 0.0))

    row = lax.broadcasted_iota(jnp.int32, (8, COLS), 0)
    column = lax.broadcasted_iota(jnp.int32, (8, COLS), 1)

    def tile_rows(tile):
        return pl.ds(pl.multiple_of(tile * 8, 8), 8)

    def neighbours(ref, colour, z, tile):
        here = tile_rows(tile)
        current = ref[z, here, :]
        before = ref[z, tile_rows(lax.rem(tile + TILES - 1, TILES)), :]
        after = ref[z, tile_rows(lax.rem(tile + 1, TILES)), :]
        minus = jnp.where(row == 0, pltpu.roll(before, 1, 0), pltpu.roll(current, 1, 0))
        plus = jnp.where(row == 7, pltpu.roll(after, 7, 0), pltpu.roll(current, 7, 0))
        even_x = (column + z) % 2 == colour
        return (
            ref[z - 1, here, :] if z > 0 else None,
            ref[z + 1, here, :] if z < BZ - 1 else None,
            current,
            jnp.where(even_x, minus, plus),
            pltpu.roll(current, 1, 1),
            pltpu.roll(current, COLS - 1, 1),
        )

    def make_faces(tile, _):
        here = tile_rows(tile)
        for colour in range(2):
            centre_ref, other_ref = (ext.at[BETA_R], ext.at[BETA_K]) if colour == 0 else (ext.at[BETA_K], ext.at[BETA_R])
            for z in range(BZ):
                centre = centre_ref[z, here, :]
                total = None
                for n, value in enumerate(neighbours(other_ref, colour, z, tile)):
                    face = 0.5 * centre if value is None else 0.5 * (centre + value)
                    if value is not None:
                        faces[colour, n, z, here, :] = face
                    total = face if total is None else total + face
                inside = centre > 0.0
                diag[colour, z, here, :] = total
                inverse[colour, z, here, :] = jnp.where(inside, 1.0 / jnp.where(inside, total, 1.0), 0.0)
        return 0

    def pulled(colour, other_ref, rhs_plane, z, tile):
        here = tile_rows(tile)
        total = ext[rhs_plane, z, here, :]
        for n, value in enumerate(neighbours(other_ref, colour, z, tile)):
            if value is not None:
                total = total + faces[colour, n, z, here, :] * value
        return total

    def update_red(tile, _):
        here = tile_rows(tile)
        for z in range(BZ):
            red[z, here, :] = pulled(0, ext.at[PHI_K], RHS_R, z, tile) * inverse[0, z, here, :]
        return 0

    own = 4 * LANES

    def black_own(tile, _):
        here = tile_rows(tile)
        for z in range(BZ):
            value = pulled(1, red, RHS_K, z, tile) * inverse[1, z, here, :]
            ext[PHI_K, z, here, :own] = value[:, :own]
        return 0

    def black_side(tile, _):
        here = tile_rows(tile)
        before, after = tile_rows(lax.rem(tile + TILES - 1, TILES)), tile_rows(lax.rem(tile + 1, TILES))
        side = slice(own, COLS)
        for z in range(BZ):
            current = red[z, here, side]
            minus = jnp.where(row[:, side] == 0, pltpu.roll(red[z, before, side], 1, 0), pltpu.roll(current, 1, 0))
            plus = jnp.where(row[:, side] == 7, pltpu.roll(red[z, after, side], 7, 0), pltpu.roll(current, 7, 0))
            even_x = (column[:, side] + z) % 2 == 1
            earlier, later = red[z, here, own - LANES : own], red[z, here, 0:LANES]
            values = (
                red[z - 1, here, side] if z > 0 else None,
                red[z + 1, here, side] if z < BZ - 1 else None,
                current,
                jnp.where(even_x, minus, plus),
                jnp.where(lane == 0, pltpu.roll(earlier, 1, 1), pltpu.roll(current, 1, 1)),
                jnp.where(lane == LANES - 1, pltpu.roll(later, LANES - 1, 1), pltpu.roll(current, LANES - 1, 1)),
            )
            total = ext[RHS_K, z, here, side]
            for n, value in enumerate(values):
                if value is not None:
                    total = total + faces[1, n, z, here, side] * value
            ext[PHI_K, z, here, side] = total * inverse[1, z, here, side]
        return 0

    def write(out, z, tile, red_part, black_part):
        even_x = (column[:, :own] + z) % 2 == 0
        start = pl.multiple_of(tile * 16, 16)
        even, odd = jnp.where(even_x, red_part, black_part), jnp.where(even_x, black_part, red_part)
        for m in range(4):
            part = slice(m * LANES, (m + 1) * LANES)
            parts[out, z, m, pl.ds(start, 8, stride=2), :] = even[:, part]
            parts[out, z, m, pl.ds(start + 1, 8, stride=2), :] = odd[:, part]

    def last_black(tile, _):
        here = tile_rows(tile)
        for z in range(BZ):
            total = pulled(1, red, RHS_K, z, tile)
            value = total * inverse[1, z, here, :]
            ext[PHI_K, z, here, :] = value
            black_res[z, here, :] = total - diag[1, z, here, :] * value
        return 0

    def outputs(tile, _):
        here = tile_rows(tile)
        for z in range(BZ):
            red_value = red[z, here, :]
            total = pulled(0, ext.at[PHI_K], RHS_R, z, tile)
            red_res = total - diag[0, z, here, :] * red_value
            write(0, z, tile, red_value[:, :own], ext[PHI_K, z, here, :][:, :own])
            write(1, z, tile, red_res[:, :own], black_res[z, here, :][:, :own])
        return 0

    for u in range(4):
        lay_out(u)
    merge(0)
    lax.fori_loop(0, TILES, make_faces, 0)
    merge(1)
    merge(2)
    lax.fori_loop(0, TILES, update_red, 0, unroll=3)
    lax.fori_loop(0, OWN_TILES, black_own, 0, unroll=2)
    merge(3)
    lax.fori_loop(0, OWN_TILES, black_side, 0, unroll=4)
    black_own(OWN_TILES, 0)
    black_side(OWN_TILES, 0)
    lax.fori_loop(0, TILES, update_red, 0, unroll=9)
    lax.fori_loop(0, TILES, last_black, 0, unroll=9)
    lax.fori_loop(0, OWN_TILES, outputs, 0, unroll=8)

    for f in range(3):
        part = s1[f].at[pl.ds(0, ND - 1)]
        pltpu.make_async_copy(part, part, s1_sem.at[f]).wait()
    for u in range(4):
        part = s2[u].at[pl.ds(0, ND - 1)]
        pltpu.make_async_copy(part, part, s2_sem.at[u]).wait()
        for copy in halo_copies(u):
            copy.wait_send()


def local(source, coefficient, initial_guess, box_place):
    vmem, dma = pltpu.VMEM, pltpu.SemaphoreType.DMA
    plane = (BZ, ROWS, COLS)
    any_spec = pl.BlockSpec(memory_space=pl.ANY)
    inputs = [pltpu.with_memory_space_constraint(x, pltpu.HBM) for x in (source, coefficient, initial_guess, box_place)]
    parts = pl.pallas_call(
        kernel,
        out_shape=jax.ShapeDtypeStruct((2, BZ, 4, 128, LANES), F32),
        in_specs=[any_spec] * 4,
        out_specs=pl.BlockSpec(memory_space=pltpu.VMEM),
        scratch_shapes=[
            vmem((3, 16, 16384), F32),
            *[vmem((ND, rows, LANES), F32) for rows in (16, 8, 16)],
            *[vmem((ND, rows, LANES), F32) for rows in (16, 8, 16)],
            vmem((2, ND * 16, LANES), F32),
            *[vmem((ND, rows, LANES), F32) for rows in (16, 8, 8, 8)],
            *[vmem((ND * rows, LANES), F32) for rows in (16, 8, 8, 8)],
            vmem((5, *plane), F32),
            vmem(plane, F32),
            vmem((2, 6, *plane), F32),
            vmem((2, *plane), F32),
            vmem((2, *plane), F32),
            vmem(plane, F32),
            vmem((5, 2, 2, 8, LANES), F32),
            vmem((5, 2, 2, 8, 4 * LANES), F32),
            vmem((5, 2, 2, 8, LANES), F32),
            vmem((5, 2, 2, 8, 4 * LANES), F32),
            vmem((5, 2, 2, 2, 8, LANES), F32),
            pltpu.SMEM((ND * 16,), jnp.int32),
            vmem((NX * 2, LANES), jnp.int32),
            pltpu.SMEM((NX * 2, LANES), jnp.int32),
            dma((3,)),
            dma((3,)),
            dma((3,)),
            dma((4,)),
            dma((4,)),
            dma((4, 8)),
            dma((4, 8)),
            dma,
            dma,
        ],
        compiler_params=pltpu.CompilerParams(
            collective_id=0, has_side_effects=True, vmem_limit_bytes=48 << 20
        ),
    )(*inputs)
    return pl.pallas_call(
        store_kernel,
        out_shape=(jax.ShapeDtypeStruct((BZ, 128, 512), F32),) * 2,
        in_specs=[any_spec],
        out_specs=(any_spec,) * 2,
        scratch_shapes=[dma((2,))],
        compiler_params=pltpu.CompilerParams(vmem_limit_bytes=4 << 20),
    )(parts)


def solution(mesh):
    boxes = P(("bx", "by"), None)
    out = P(None, "bx", "by")
    return jax.shard_map(
        local,
        mesh=mesh,
        in_specs=(boxes, boxes, boxes, P()),
        out_specs=(out, out),
        check_vma=False,
    )
```
